32 devices in a mesh: groups: 2 (over x), seq: 16 (over z, y, core).
Axes of the slice: x: 2, y: 2, z: 4, core: 2. Of those that a mesh axis runs over, the one named last changes fastest.
Arguments:
- queries: bfloat16 [4096, 2560], P(('groups', 'seq')), parts along dimension 0, may hold values from -12 to 12
- key_vectors: bfloat16 [4096, 2560], P(('groups', 'seq')), parts along dimension 0, may hold values from -6 to 6
- value_vectors: bfloat16 [4096, 2560], P(('groups', 'seq')), parts along dimension 0, may hold values from -6 to 6
- step_sizes: float32 [4096, 8], P(('groups', 'seq')), parts along dimension 0, may hold values from 0.02 to 0.3
- fast_weights: float32 [320, 7680], P('seq'), may hold values from -20 to 20
- fast_gain: float32 [2560], replicated, may hold values from 0.25 to 1.75
- window_gain: float32 [2560], replicated, may hold values from 0.25 to 1.75
Outputs:
- layer_out: bfloat16 [4096, 2560], P(('groups', 'seq')), parts along dimension 0
- new_weights: float32 [640, 7680], P(('groups', 'seq')), parts along dimension 0
- momentum: float32 [640, 7680], P(('groups', 'seq')), parts along dimension 0
The draws below stay inside these ranges and needn't reach their ends.
There are 2 independent parts, one for each index of `groups`. The reference program is written for one: setup_inputs(seed, part) draws one part's arguments, and reference() takes and returns one part's arrays. A program takes and returns all parts, laid end to end along the dimension named above; an argument that names none is the same for every part. Nothing has to cross between parts.
All inputs are finite; a program needn't handle non-finite values.
Results may differ from the reference program's by a relative error of at most 0.0066.
Values may be sent and summed in bfloat16 or wider, within the bound.
No kernel may reach another device: no remote copies, remote signals or barrier semaphores. Data moves between devices by JAX's collectives and lax.ppermute only.
A program may use at most 128 MiB of HBM per device.

```python
import math
import jax
import jax.numpy as jnp
from jax import lax

H = 8
DH = 320
WINDOW = 1024
BLOCK = 2048


def draw_queries(key, part):
    return jnp.clip(jax.random.normal(jax.random.fold_in(key, 1), (BLOCK, H * DH)), -6.0, 6.0).astype(jnp.bfloat16)


def draw_key_vectors(key, part):
    return jnp.clip(jax.random.normal(jax.random.fold_in(key, 2), (BLOCK, H * DH)), -6.0, 6.0).astype(jnp.bfloat16)


def draw_fast_weights(key, part):
    columns = 3 * H * DH
    rising = (3.0 ** (jnp.arange(DH, dtype=jnp.float32) / (DH - 1)))[:, None]
    entries = jnp.clip(jax.random.normal(jax.random.fold_in(key, 1), (DH, columns)), -4.0, 4.0)
    row_factor = 0.5 * rising * jnp.exp(jax.random.uniform(jax.random.fold_in(key, 2), (DH, 1), minval=-0.7, maxval=0.7))
    col_factor = jnp.exp(jax.random.uniform(jax.random.fold_in(key, 3), (1, columns), minval=-1.15, maxval=1.15))
    return jnp.clip(entries * row_factor * col_factor, -20.0, 20.0)


def shard_levels(rng, shape, shards, smallest, largest):
    def one(position, parts):
        steps = jax.random.uniform(jax.random.fold_in(jax.random.fold_in(rng, 6), position), (parts,), jnp.float32, smallest / len(shards), largest / len(shards))
        return jnp.repeat(jnp.exp(steps), shape[position] // parts).reshape((-1,) + (1,) * (len(shape) - position - 1))

    factor_of = one(*shards[0])
    for cut in shards[1:]:
        factor_of = factor_of * one(*cut)
    return factor_of


def gaussian(key, dims, deviation, reach, split=(), kind=jnp.bfloat16):
    values = deviation * jax.random.normal(key, dims, jnp.float32)
    if split:
        values = values * shard_levels(key, dims, split, -0.22, 0.18)
    return jnp.clip(values, -reach, reach).astype(kind)


def setup_inputs(seed: int = 0, part: int = 0) -> dict:
    key_list = jax.random.split(jax.random.key(seed), 8)
    own_keys = jax.random.split(jax.random.fold_in(key_list[7], part), 8)
    return {
        "queries": draw_queries(jax.random.fold_in(jax.random.fold_in(key_list[7], part), 71), part),
        "key_vectors": draw_key_vectors(jax.random.fold_in(jax.random.fold_in(key_list[7], part), 71), part),
        "value_vectors": gaussian(own_keys[2], (BLOCK, H * DH), 1.0, 6.0, ((0, 16),)),
        "step_sizes": jnp.clip(jnp.exp(math.log(0.3) - 2.7080503 * jax.random.uniform(own_keys[3], (BLOCK, H), jnp.float32) ** shard_levels(own_keys[3], (BLOCK, H), ((0, 16),), -0.2, 0.2)), 0.02, 0.3),
        "fast_weights": draw_fast_weights(jax.random.fold_in(key_list[7], 71), part),
        "fast_gain": jnp.clip(1.0 + 0.15 * jax.random.normal(key_list[5], (H * DH,), jnp.float32), 0.25, 1.75),
        "window_gain": jnp.clip(1.0 + 0.15 * jax.random.normal(key_list[6], (H * DH,), jnp.float32), 0.25, 1.75),
    }


def normalize(field, gain_row):
    mean_sq = lax.optimization_barrier(jnp.mean(field * field, axis=-1, keepdims=True))
    return field * lax.rsqrt(mean_sq + 1e-05) * gain_row

def silu_slope(gate):
    sigma = jax.nn.sigmoid(gate)
    return sigma * (1.0 + gate * (1.0 - sigma))

def reference(queries, key_vectors, value_vectors, step_sizes, fast_weights, fast_gain, window_gain):
    score_scale = 1.0 / math.sqrt(DH)
    copies = fast_weights.astype(jnp.bfloat16).reshape(DH, 3, H, DH)
    w_first = copies[:, 0]
    w_third = copies[:, 1]
    w_second = copies[:, 2]
    query_heads = queries.reshape(BLOCK, H, DH)
    key_heads = key_vectors.reshape(BLOCK, H, DH)
    value_heads = value_vectors.reshape(BLOCK, H, DH)

    def project(inputs, matrix):
        return jnp.einsum('thr,rhc->thc', inputs.astype(jnp.float32), matrix.astype(jnp.float32)) * score_scale
    gate_query = project(query_heads, w_first)
    up_query = project(query_heads, w_third)
    hidden_query = (jax.nn.silu(gate_query) * up_query).astype(jnp.bfloat16)
    fast_part = normalize(project(hidden_query, w_second), fast_gain.reshape(H, DH))
    padding = jnp.zeros((WINDOW, H * DH), jnp.bfloat16)
    padded_keys = jnp.concatenate([padding, key_vectors], axis=0)
    padded_values = jnp.concatenate([padding, value_vectors], axis=0)

    def window_block(block_index):
        begin = block_index * WINDOW
        query_block = lax.dynamic_slice_in_dim(queries, begin, WINDOW, 0).reshape(WINDOW, H, DH)
        key_block = lax.dynamic_slice_in_dim(padded_keys, begin, 2 * WINDOW, 0).reshape(2 * WINDOW, H, DH)
        value_block = lax.dynamic_slice_in_dim(padded_values, begin, 2 * WINDOW, 0).reshape(2 * WINDOW, H, DH)
        query_pos = begin + jnp.arange(WINDOW, dtype=jnp.int32)
        key_pos = begin - WINDOW + jnp.arange(2 * WINDOW, dtype=jnp.int32)
        distance = query_pos[:, None] - key_pos[None, :]
        allowed = (distance >= 0) & (distance < WINDOW) & (key_pos[None, :] >= 0)
        scores = jnp.einsum('qhd,khd->hqk', query_block.astype(jnp.float32), key_block.astype(jnp.float32)) * score_scale
        scores = jnp.where(allowed[None], scores, -jnp.inf)
        row_max = lax.optimization_barrier(jnp.max(scores, axis=-1, keepdims=True))
        weights = jnp.exp(scores - row_max)
        attention_probs = (weights / lax.optimization_barrier(jnp.sum(weights, axis=-1, keepdims=True))).astype(jnp.bfloat16)
        return jnp.einsum('hqk,khd->qhd', attention_probs.astype(jnp.float32), value_block.astype(jnp.float32))
    attended = lax.map(window_block, jnp.arange(BLOCK // WINDOW, dtype=jnp.int32)).reshape(BLOCK, H, DH)
    window_part = normalize(attended, window_gain.reshape(H, DH))
    layer_out = (fast_part + window_part).astype(jnp.bfloat16).reshape(BLOCK, H * DH)
    gate_key = project(key_heads, w_first)
    up_key = project(key_heads, w_third)
    hidden_key = (jax.nn.silu(gate_key) * up_key).astype(jnp.bfloat16)
    target = (-step_sizes[:, :, None] * value_heads.astype(jnp.float32)).astype(jnp.bfloat16)
    back_hidden = jnp.einsum('thc,rhc->thr', target.astype(jnp.float32), w_second.astype(jnp.float32)) * score_scale
    grad_gate = (back_hidden * up_key * silu_slope(gate_key)).astype(jnp.bfloat16)
    grad_up = (back_hidden * jax.nn.silu(gate_key)).astype(jnp.bfloat16)
    key_float = key_heads.astype(jnp.float32)
    first = jnp.einsum('thr,thc->rhc', key_float, grad_gate.astype(jnp.float32))
    third = jnp.einsum('thr,thc->rhc', key_float, grad_up.astype(jnp.float32))
    second = jnp.einsum('thr,thc->rhc', hidden_key.astype(jnp.float32), target.astype(jnp.float32))
    momentum = jnp.stack([first, third, second], axis=1).reshape(DH, 3 * H * DH) * score_scale
    moved = fast_weights - momentum
    old_sum = lax.optimization_barrier(jnp.sum(fast_weights * fast_weights, axis=0))
    new_sum = lax.optimization_barrier(jnp.sum(moved * moved, axis=0))
    new_weights = moved * jnp.sqrt((old_sum + 1e-06) / (new_sum + 1e-06))
    return (layer_out, new_weights, momentum)
```

```python
import functools
import math

import jax
import jax.numpy as jnp
from jax import lax
from jax.experimental import pallas as pl
from jax.experimental.pallas import tpu as pltpu
from jax.sharding import PartitionSpec as P

WINDOW = 1024
LANES = 128
HALF = 64
VMEM_LIMIT = 48 * 1024 * 1024
BF16 = jnp.bfloat16
F32 = jnp.float32
ORDER = (4, 5, 6, 7, 2, 3, 1)
ANY = pl.BlockSpec(memory_space=pl.ANY)
VMEM = pl.BlockSpec(memory_space=pltpu.VMEM)


def tiles_of(head):
    first = (5 * head) // 2
    odd = head % 2
    return (first + odd) * LANES, (first if odd else first + 2) * LANES


def turned(tile):
    return pltpu.roll(tile, HALF, axis=1)


def low_lanes(rows):
    return lax.broadcasted_iota(jnp.int32, (rows, LANES), 1) < HALF


def dot(left, right, contract):
    return lax.dot_general(left, right, (contract, ((), ())), preferred_element_type=F32)


def chip_core(width):
    place = lax.axis_index("seq")
    return place // width, lax.rem(place, width)


def copy_all(pairs, sems):
    copies = [pltpu.make_async_copy(src, dst, sems.at[i]) for i, (src, dst) in enumerate(pairs)]
    for copy in copies:
        copy.start()
    return copies


def pack_keys(width, heads, rows, slot, k_ref, v_ref, step_ref, fw_ref, *rest):
    outs, (pay, wbuf, sems) = rest[:heads], rest[heads:]
    chip, _ = chip_core(width)
    tokens = k_ref.shape[0]
    low = low_lanes(tokens)
    low_r = low_lanes(rows)
    matrix = fw_ref.shape[1] // 3
    steps = step_ref[...].T
    high = steps.astype(BF16).astype(F32)
    middle = (steps - high).astype(BF16).astype(F32)
    rest_ = (steps - high - middle).astype(BF16).astype(F32)
    wbuf[...] = jnp.zeros_like(wbuf)
    for head in range(heads):
        whole, half = tiles_of(head)
        odd = head % 2
        pay[head, 0:tokens] = k_ref[:, whole : whole + LANES]
        pay[head, tokens : 2 * tokens] = k_ref[:, whole + LANES : whole + 2 * LANES]
        pay[head, 3 * tokens : 4 * tokens] = v_ref[:, whole : whole + LANES]
        pay[head, 4 * tokens : 5 * tokens] = v_ref[:, whole + LANES : whole + 2 * LANES]
        k_half = k_ref[:, half : half + LANES].astype(F32)
        v_half = v_ref[:, half : half + LANES].astype(F32)
        mixed = jnp.where(low, turned(k_half) if odd else k_half, v_half if odd else turned(v_half))
        pay[head, 2 * tokens : 3 * tokens] = mixed.astype(BF16)
        halves = []
        for m in range(3):
            base = m * matrix
            for t in range(2):
                at = (2 * m + t) * slot
                lane = base + whole + t * LANES
                wbuf[at : at + rows] = fw_ref[:, lane : lane + LANES]
            halves.append(fw_ref[:, base + half : base + half + LANES])
        first, third, second = halves
        if odd:
            first, third = turned(first), turned(third)
        else:
            second = turned(second)
        wbuf[6 * slot : 6 * slot + rows] = jnp.where(low_r, first, second)
        wbuf[7 * slot : 7 * slot + rows] = jnp.where(low_r, third, 0.0)
        wbuf[rows : rows + 1] = high[head : head + 1]
        wbuf[rows + 1 : rows + 2] = middle[head : head + 1]
        wbuf[rows + 2 : rows + 3] = rest_[head : head + 1]
        pay[head, 5 * tokens :] = wbuf[...].astype(BF16)
    for copy in copy_all([(pay.at[chip ^ k], outs[k]) for k in range(heads)], sems):
        copy.wait()


def pack_queries(width, heads, q_ref, *rest):
    outs, (pay, sems) = rest[:heads], rest[heads:]
    chip, _ = chip_core(width)
    tokens = q_ref.shape[0]
    mid = tokens // 2
    low = low_lanes(mid)
    for head in range(heads):
        whole, half = tiles_of(head)
        pay[head, 0:tokens] = q_ref[:, whole : whole + LANES]
        pay[head, tokens : 2 * tokens] = q_ref[:, whole + LANES : whole + 2 * LANES]
        top = q_ref[0:mid, half : half + LANES].astype(F32)
        bottom = q_ref[mid:, half : half + LANES].astype(F32)
        if head % 2:
            top = turned(top)
        else:
            bottom = turned(bottom)
        pay[head, 2 * tokens :] = jnp.where(low, top, bottom).astype(BF16)
    for copy in copy_all([(pay.at[chip ^ k], outs[k]) for k in range(heads)], sems):
        copy.wait()


def key_side(width, heads, rows, slot, tokens, scale, *refs):
    count = heads * width
    ins = refs[: count]
    grad_ref, copy_ref, nat_ref = refs[count : count + 3]
    buf, wbuf, natural, gates, hidden, target, sems = refs[count + 3 :]
    chip, core = chip_core(width)
    pairs = []
    for other in range(width):
        for k in range(heads):
            source = (chip ^ k) * width + (core ^ other)
            src = ins[other * heads + k]
            if other == 0:
                pairs.append((src, buf.at[source]))
            else:
                pairs.append((src.at[pl.ds(5 * tokens, 8 * slot)], buf.at[source, pl.ds(5 * tokens, 8 * slot)]))
    for copy in copy_all(pairs, sems):
        copy.wait()
    wide = 3 * LANES
    width_of = rows * count
    low = low_lanes(rows)
    for source in range(count):
        wbuf[...] = buf[source, 5 * tokens :].astype(F32)
        at = source * rows
        for m in range(2):
            for t in range(2):
                natural[at : at + rows, m * wide + t * LANES : m * wide + (t + 1) * LANES] = wbuf[
                    (2 * m + t) * slot : (2 * m + t) * slot + rows
                ]
        for t in range(2):
            natural[at : at + rows, 2 * wide + (t + 1) * LANES : 2 * wide + (t + 2) * LANES] = wbuf[
                (4 + t) * slot : (4 + t) * slot + rows
            ]
        both = wbuf[6 * slot : 6 * slot + rows]
        natural[at : at + rows, 2 * LANES : 3 * LANES] = jnp.where(low, both, 0.0)
        natural[at : at + rows, 2 * wide : 2 * wide + LANES] = jnp.where(low, 0.0, both)
        natural[at : at + rows, wide + 2 * LANES : wide + 3 * LANES] = wbuf[7 * slot : 7 * slot + rows]
    nat_ref[...] = natural[...].astype(BF16)
    odd = lax.rem(chip, 2)
    copy_ref[0 : 2 * LANES] = natural[pl.ds(pl.multiple_of(odd * HALF, HALF), 2 * LANES)].astype(BF16)
    copy_ref[2 * LANES : 2 * LANES + HALF] = natural[
        pl.ds(pl.multiple_of((1 - odd) * 2 * LANES, HALF), HALF)
    ].astype(BF16)
    copy_ref[width_of:] = jnp.zeros((copy_ref.shape[0] - width_of, copy_ref.shape[1]), BF16)

    steps = [
        jnp.sum(buf[j * width + core, 5 * tokens : 5 * tokens + slot].astype(F32)[rows : rows + 3], axis=0, keepdims=True)
        for j in range(heads)
    ]
    steps = jnp.concatenate(steps, axis=0).T
    w13 = copy_ref[:, 0 : 2 * wide]
    w2 = copy_ref[:, 2 * wide :]
    for j in range(heads):
        block = buf[j * width + core, 0 : 5 * tokens]
        keys = jnp.concatenate([block[0:tokens], block[tokens : 2 * tokens], block[2 * tokens : 3 * tokens]], axis=1)
        values = jnp.concatenate(
            [block[2 * tokens : 3 * tokens], block[3 * tokens : 4 * tokens], block[4 * tokens :]], axis=1
        )
        at = j * tokens
        tgt = (-steps[:, j : j + 1] * values.astype(F32)).astype(BF16)
        both = dot(keys, w13, ((1,), (0,))) * scale
        back = dot(tgt, w2, ((1,), (1,))) * scale
        gate, up = both[:, :wide], both[:, wide:]
        sig = 1.0 / (1.0 + jnp.exp(-gate))
        silu = gate * sig
        gates[at : at + tokens, 0:wide] = (back * up * (sig * (1.0 + gate * (1.0 - sig)))).astype(BF16)
        gates[at : at + tokens, wide:] = (back * silu).astype(BF16)
        hidden[at : at + tokens] = (silu * up).astype(BF16)
        target[at : at + tokens] = tgt
    all_keys = jnp.concatenate(
        [
            jnp.concatenate([buf[j * width + core, t * tokens : (t + 1) * tokens] for t in range(3)], axis=1)
            for j in range(heads)
        ],
        axis=0,
    )
    grads13 = dot(all_keys, gates[...], ((0,), (0,))) * scale
    grads2 = dot(hidden[...], target[...], ((0,), (0,))) * scale
    first_row = pl.multiple_of(odd * HALF, HALF)
    last_row = pl.multiple_of((1 - odd) * 2 * LANES, HALF)
    grad_ref[pl.ds(first_row, 2 * LANES), 0 : 2 * wide] = grads13[0 : 2 * LANES]
    grad_ref[pl.ds(last_row, HALF), 0 : 2 * wide] = grads13[2 * LANES : 2 * LANES + HALF]
    grad_ref[pl.ds(first_row, 2 * LANES), 2 * wide :] = grads2[0 : 2 * LANES]
    grad_ref[pl.ds(last_row, HALF), 2 * wide :] = grads2[2 * LANES : 2 * LANES + HALF]


def query_side(width, heads, tokens, scale, span, *refs):
    count = heads * width
    kv = refs[:count]
    qs = refs[count : count + heads]
    copy_ref, fast_gain_ref, window_gain_ref = refs[count + heads : count + heads + 3]
    outs = refs[count + heads + 3 : count + 2 * heads + 3]
    buf, qbuf, pay, sems, out_sems = refs[count + 2 * heads + 3 :]
    chip, core = chip_core(width)
    pairs = []
    for other in range(width):
        for k in range(heads):
            source = (chip ^ k) * width + (core ^ other)
            pairs.append((kv[other * heads + k].at[pl.ds(0, 5 * tokens)], buf.at[source]))
    for k in range(heads):
        pairs.append((qs[k], qbuf.at[chip ^ k]))
    for copy in copy_all(pairs, sems):
        copy.wait()
    wide = 3 * LANES
    mid = tokens // 2
    low = low_lanes(mid)
    high = jnp.logical_not(low_lanes(tokens))
    size = heads * 40
    w13 = copy_ref[:, 0 : 2 * wide]
    w2 = copy_ref[:, 2 * wide :]
    fast_gain = fast_gain_ref[...]
    window_gain = window_gain_ref[...]
    keys_seen = (span + 1) * tokens
    ahead = lax.broadcasted_iota(jnp.int32, (tokens, keys_seen), 0) - lax.broadcasted_iota(
        jnp.int32, (tokens, keys_seen), 1
    )
    for j in range(heads):
        place = j * width + core
        start = jnp.maximum(place - span, 0)
        q_tail = qbuf[j, 2 * tokens :].astype(F32)
        q_half = jnp.concatenate([jnp.where(low, q_tail, 0.0), jnp.where(low, turned(q_tail), 0.0)], axis=0)
        q = jnp.concatenate([qbuf[j, 0:tokens], qbuf[j, tokens : 2 * tokens], q_half.astype(BF16)], axis=1)
        seen = buf[pl.ds(start, span + 1)]
        tiles = [seen[:, t * tokens : (t + 1) * tokens].reshape(keys_seen, LANES) for t in range(5)]
        score = dot(q, jnp.concatenate(tiles[0:3], axis=1), ((1,), (1,)))
        distance = ahead + (place - start) * tokens
        score = jnp.where((distance >= 0) & (distance < span * tokens), score, -jnp.inf)
        top = jnp.max(score, axis=1, keepdims=True)
        weight = jnp.exp2((score - top) * (scale * math.log2(math.e)))
        total = jnp.sum(weight, axis=1, keepdims=True)
        attended = dot(weight.astype(BF16), jnp.concatenate(tiles[2:5], axis=1), ((1,), (0,))) / total
        attended = jnp.concatenate([jnp.where(high, attended[:, 0:LANES], 0.0), attended[:, LANES:]], axis=1)
        mean_sq = jnp.sum(attended * attended, axis=1, keepdims=True) * (1.0 / size)
        window_part = attended * lax.rsqrt(mean_sq + 1e-05) * window_gain

        both = dot(q, w13, ((1,), (0,))) * scale
        gate, up = both[:, :wide], both[:, wide:]
        hid = (gate / (1.0 + jnp.exp(-gate)) * up).astype(BF16)
        out = dot(hid, w2, ((1,), (0,))) * scale
        mean_sq = jnp.sum(out * out, axis=1, keepdims=True) * (1.0 / size)
        layer = out * lax.rsqrt(mean_sq + 1e-05) * fast_gain + window_part
        pay[j, 0:tokens] = layer[:, LANES : 2 * LANES].astype(BF16)
        pay[j, tokens : 2 * tokens] = layer[:, 2 * LANES :].astype(BF16)
        pay[j, 2 * tokens :] = jnp.where(low, turned(layer[mid:, 0:LANES]), layer[0:mid, 0:LANES]).astype(BF16)
    for copy in copy_all([(pay.at[chip ^ k], outs[k]) for k in range(heads)], out_sems):
        copy.wait()


def pack_momentum(width, heads, rows, slot, mine_ref, *refs):
    others = refs[: width - 1]
    nat_ref = refs[width - 1]
    outs = refs[width : width + heads]
    total, scales, pieces, wbuf, pay, sems = refs[width + heads :]
    chip, core = chip_core(width)
    summed = mine_ref[...]
    for other in others:
        summed = summed + other[...]
    summed = summed.astype(BF16).astype(F32)
    total[...] = summed
    old = nat_ref[...].astype(F32)
    moved = old - summed
    ratio = (jnp.sum(old * old, axis=0, keepdims=True) + 1e-06) / (jnp.sum(moved * moved, axis=0, keepdims=True) + 1e-06)
    ratio = jnp.sqrt(ratio)
    high = ratio.astype(BF16).astype(F32)
    scales[0:1] = high
    scales[1:2] = ratio - high
    wide = 3 * LANES
    low = low_lanes(rows)
    low_1 = low_lanes(2)
    for source in range(heads * width):
        pieces[source, 0:rows] = total[source * rows : (source + 1) * rows]
    wbuf[...] = jnp.zeros_like(wbuf)
    for head in range(heads):
        source = head * width + core
        for m in range(3):
            for t in range(2):
                lane = m * wide + t * LANES + (LANES if m == 2 else 0)
                at = (2 * m + t) * slot
                wbuf[at : at + rows] = pieces[source, 0:rows, lane : lane + LANES]
                wbuf[at + rows : at + rows + 2] = scales[0:2, lane : lane + LANES]
        at = 6 * slot
        wbuf[at : at + rows] = jnp.where(
            low, pieces[source, 0:rows, 2 * LANES : 3 * LANES], pieces[source, 0:rows, 2 * wide : 2 * wide + LANES]
        )
        wbuf[at + rows : at + rows + 2] = jnp.where(
            low_1, scales[0:2, 2 * LANES : 3 * LANES], scales[0:2, 2 * wide : 2 * wide + LANES]
        )
        at = 7 * slot
        wbuf[at : at + rows] = pieces[source, 0:rows, wide + 2 * LANES : wide + 3 * LANES]
        wbuf[at + rows : at + rows + 2] = scales[0:2, wide + 2 * LANES : wide + 3 * LANES]
        pay[head] = wbuf[...].astype(BF16)
    for copy in copy_all([(pay.at[chip ^ k], outs[k]) for k in range(heads)], sems):
        copy.wait()


def unpack(width, heads, rows, slot, tokens, *refs):
    layers = refs[:heads]
    moments = refs[heads : 2 * heads]
    fw_ref, layer_ref, new_ref, momentum_ref, lbuf, mbuf, wbuf, sems = refs[2 * heads :]
    chip, _ = chip_core(width)
    pairs = [(layers[k], lbuf.at[chip ^ k]) for k in range(heads)]
    pairs += [(moments[k], mbuf.at[chip ^ k]) for k in range(heads)]
    for copy in copy_all(pairs, sems):
        copy.wait()
    mid = tokens // 2
    low = low_lanes(mid)
    low_r = low_lanes(slot)
    matrix = fw_ref.shape[1] // 3

    def write(lane, block):
        moment = block[0:rows]
        factor = block[rows : rows + 1] + block[rows + 1 : rows + 2]
        momentum_ref[:, lane : lane + LANES] = moment
        new_ref[:, lane : lane + LANES] = (fw_ref[:, lane : lane + LANES] - moment) * factor

    for head in range(heads):
        whole, half = tiles_of(head)
        layer_ref[:, whole : whole + LANES] = lbuf[head, 0:tokens]
        layer_ref[:, whole + LANES : whole + 2 * LANES] = lbuf[head, tokens : 2 * tokens]
        wbuf[head] = mbuf[head].astype(F32)
        for m in range(3):
            for t in range(2):
                write(m * matrix + whole + t * LANES, wbuf[head, (2 * m + t) * slot : (2 * m + t + 1) * slot])
    for head in range(0, heads, 2):
        _, half = tiles_of(head)
        even = lbuf[head, 2 * tokens :].astype(F32)
        odd = lbuf[head + 1, 2 * tokens :].astype(F32)
        layer_ref[0:mid, half : half + LANES] = jnp.where(low, turned(even), odd).astype(BF16)
        layer_ref[mid:, half : half + LANES] = jnp.where(low, even, turned(odd)).astype(BF16)
        even = wbuf[head, 6 * slot : 7 * slot]
        odd = wbuf[head + 1, 6 * slot : 7 * slot]
        write(half, jnp.where(low_r, even, turned(odd)))
        write(2 * matrix + half, jnp.where(low_r, turned(even), odd))
        even = wbuf[head, 7 * slot :]
        odd = wbuf[head + 1, 7 * slot :]
        write(matrix + half, jnp.where(low_r, even, turned(odd)))


def shards(queries, key_vectors, value_vectors, step_sizes, fast_weights, fast_gain, window_gain):
    tokens = queries.shape[0]
    heads = step_sizes.shape[1]
    head_width = queries.shape[1] // heads
    scale = 1.0 / math.sqrt(head_width)
    count = lax.axis_size("seq")
    width = count // heads
    rows = fast_weights.shape[0]
    slot = -(-(rows + 3) // 8) * 8
    span = WINDOW // tokens
    wide = 3 * LANES
    params = pltpu.CompilerParams(vmem_limit_bytes=VMEM_LIMIT)
    sem = pltpu.SemaphoreType.DMA
    key_rows = 5 * tokens + 8 * slot
    query_rows = 2 * tokens + tokens // 2

    def across(value, step):
        return lax.ppermute(value, "seq", [(i, i ^ step) for i in range(count)])

    def exchange(pieces):
        got = {0: pieces[0]}
        for k in ORDER:
            got[k] = across(pieces[k], k * width)
        return [got[k] for k in range(heads)]

    def packed(size):
        return [jax.ShapeDtypeStruct((size, LANES), BF16)] * heads

    key_pieces = pl.pallas_call(
        functools.partial(pack_keys, width, heads, rows, slot),
        out_shape=packed(key_rows),
        in_specs=[VMEM] * 4,
        out_specs=[ANY] * heads,
        scratch_shapes=[
            pltpu.VMEM((heads, key_rows, LANES), BF16),
            pltpu.VMEM((8 * slot, LANES), F32),
            sem((heads,)),
        ],
        compiler_params=params,
        name="pack_keys",
    )(key_vectors, value_vectors, step_sizes, fast_weights)
    query_pieces = pl.pallas_call(
        functools.partial(pack_queries, width, heads),
        out_shape=packed(query_rows),
        in_specs=[VMEM],
        out_specs=[ANY] * heads,
        scratch_shapes=[pltpu.VMEM((heads, query_rows, LANES), BF16), sem((heads,))],
        compiler_params=params,
        name="pack_queries",
    )(queries)
    key_blocks = exchange(key_pieces)
    for other in range(1, width):
        key_blocks = key_blocks + [across(key_blocks[k], other) for k in range(heads)]
    query_blocks = exchange(query_pieces)

    gradient, copies, natural = pl.pallas_call(
        functools.partial(key_side, width, heads, rows, slot, tokens, scale),
        out_shape=[
            jax.ShapeDtypeStruct((head_width, 3 * wide), F32),
            jax.ShapeDtypeStruct((wide, 3 * wide), BF16),
            jax.ShapeDtypeStruct((head_width, 3 * wide), BF16),
        ],
        in_specs=[ANY] * count,
        out_specs=[VMEM] * 3,
        scratch_shapes=[
            pltpu.VMEM((count, key_rows, LANES), BF16),
            pltpu.VMEM((8 * slot, LANES), F32),
            pltpu.VMEM((head_width, 3 * wide), F32),
            pltpu.VMEM((heads * tokens, 2 * wide), BF16),
            pltpu.VMEM((heads * tokens, wide), BF16),
            pltpu.VMEM((heads * tokens, wide), BF16),
            sem((count,)),
        ],
        compiler_params=params,
        name="key_side",
    )(*key_blocks)
    gradients = [across(gradient, other) for other in range(1, width)]

    head = lax.axis_index("seq") // width
    odd = head % 2

    def gain_row(gain):
        row = lax.dynamic_slice_in_dim(gain.reshape(heads, head_width), head, 1, 0)
        gap = jnp.zeros((1, HALF), F32)
        even_row = jnp.concatenate([gap, row[:, 2 * LANES :], row[:, : 2 * LANES]], axis=1)
        odd_row = jnp.concatenate([gap, row], axis=1)
        return jnp.where(odd == 1, odd_row, even_row)

    layer_pieces = pl.pallas_call(
        functools.partial(query_side, width, heads, tokens, scale, span),
        out_shape=packed(query_rows),
        in_specs=[ANY] * (count + heads) + [VMEM] * 3,
        out_specs=[ANY] * heads,
        scratch_shapes=[
            pltpu.VMEM((count, 5 * tokens, LANES), BF16),
            pltpu.VMEM((heads, query_rows, LANES), BF16),
            pltpu.VMEM((heads, query_rows, LANES), BF16),
            sem((count + heads,)),
            sem((heads,)),
        ],
        compiler_params=params,
        name="query_side",
    )(*key_blocks, *query_blocks, copies, gain_row(fast_gain), gain_row(window_gain))

    momentum_pieces = pl.pallas_call(
        functools.partial(pack_momentum, width, heads, rows, slot),
        out_shape=packed(8 * slot),
        in_specs=[VMEM] * (width + 1),
        out_specs=[ANY] * heads,
        scratch_shapes=[
            pltpu.VMEM((head_width, 3 * wide), F32),
            pltpu.VMEM((8, 3 * wide), F32),
            pltpu.VMEM((count, slot, 3 * wide), F32),
            pltpu.VMEM((8 * slot, LANES), F32),
            pltpu.VMEM((heads, 8 * slot, LANES), BF16),
            sem((heads,)),
        ],
        compiler_params=params,
        name="pack_momentum",
    )(gradient, *gradients, natural)
    moments = exchange(momentum_pieces)
    layers = exchange(layer_pieces)

    layer_out, new_weights, momentum = pl.pallas_call(
        functools.partial(unpack, width, heads, rows, slot, tokens),
        out_shape=[
            jax.ShapeDtypeStruct(queries.shape, BF16),
            jax.ShapeDtypeStruct(fast_weights.shape, F32),
            jax.ShapeDtypeStruct(fast_weights.shape, F32),
        ],
        in_specs=[ANY] * (2 * heads) + [VMEM],
        out_specs=[VMEM] * 3,
        scratch_shapes=[
            pltpu.VMEM((heads, query_rows, LANES), BF16),
            pltpu.VMEM((heads, 8 * slot, LANES), BF16),
            pltpu.VMEM((heads, 8 * slot, LANES), F32),
            sem((2 * heads,)),
        ],
        compiler_params=params,
        name="unpack",
    )(*layers, *moments, fast_weights)
    return (layer_out, new_weights, momentum)


def solution(mesh):
    in_specs = (
        P(("groups", "seq"), None),
        P(("groups", "seq"), None),
        P(("groups", "seq"), None),
        P(("groups", "seq"), None),
        P("seq", None),
        P(),
        P(),
    )
    out_specs = (P(("groups", "seq"), None), P(("groups", "seq"), None), P(("groups", "seq"), None))
    return jax.shard_map(shards, mesh=mesh, in_specs=in_specs, out_specs=out_specs, check_vma=False)
```

```python
import functools
import math

import jax
import jax.numpy as jnp
from jax import lax
from jax.experimental import pallas as pl
from jax.experimental.pallas import tpu as pltpu
from jax.sharding import PartitionSpec as P

WINDOW = 1024
LANES = 128
HALF = 64
VMEM_LIMIT = 24 * 1024 * 1024
BF16 = jnp.bfloat16
F32 = jnp.float32
FAR_FIRST = (4, 5, 6, 7, 2, 3, 1, 0)
ANY = pl.BlockSpec(memory_space=pl.ANY)
VMEM = pl.BlockSpec(memory_space=pltpu.VMEM)


def tiles_of(head):
    first = (5 * head) // 2
    odd = head % 2
    return (first + odd) * LANES, (first if odd else first + 2) * LANES


def turned(tile):
    return pltpu.roll(tile, HALF, axis=1)


def low_lanes(rows):
    return lax.broadcasted_iota(jnp.int32, (rows, LANES), 1) < HALF


def dot(left, right, contract):
    return lax.dot_general(left, right, (contract, ((), ())), preferred_element_type=F32)


def chip_core(width):
    place = lax.axis_index("seq")
    return place // width, lax.rem(place, width)


def copy_all(pairs, sems):
    copies = [pltpu.make_async_copy(src, dst, sems.at[i]) for i, (src, dst) in enumerate(pairs)]
    for copy in copies:
        copy.start()
    return copies


def pack_keys(width, heads, rows, slot, k_ref, v_ref, step_ref, fw_ref, *rest):
    outs, (pay, wbuf, sems) = rest[:heads], rest[heads:]
    chip, _ = chip_core(width)
    tokens = k_ref.shape[0]
    low = low_lanes(tokens)
    low_r = low_lanes(rows)
    matrix = fw_ref.shape[1] // 3
    steps = step_ref[...]
    high = steps.astype(BF16).astype(F32)
    middle = (steps - high).astype(BF16).astype(F32)
    rest_ = (steps - high - middle).astype(BF16).astype(F32)
    wbuf[...] = jnp.zeros_like(wbuf)
    for head in range(heads):
        whole, half = tiles_of(head)
        odd = head % 2
        pay[head, 0:tokens] = k_ref[:, whole : whole + LANES]
        pay[head, tokens : 2 * tokens] = k_ref[:, whole + LANES : whole + 2 * LANES]
        pay[head, 3 * tokens : 4 * tokens] = v_ref[:, whole : whole + LANES]
        pay[head, 4 * tokens : 5 * tokens] = v_ref[:, whole + LANES : whole + 2 * LANES]
        k_half = k_ref[:, half : half + LANES].astype(F32)
        v_half = v_ref[:, half : half + LANES].astype(F32)
        mixed = jnp.where(low, turned(k_half) if odd else k_half, v_half if odd else turned(v_half))
        pay[head, 2 * tokens : 3 * tokens] = mixed.astype(BF16)
        halves = []
        for m in range(3):
            base = m * matrix
            for t in range(2):
                at = (2 * m + t) * slot
                lane = base + whole + t * LANES
                wbuf[at : at + rows] = fw_ref[:, lane : lane + LANES]
            halves.append(fw_ref[:, base + half : base + half + LANES])
        first, third, second = halves
        if odd:
            first, third = turned(first), turned(third)
        else:
            second = turned(second)
        wbuf[6 * slot : 6 * slot + rows] = jnp.where(low_r, first, second)
        wbuf[7 * slot : 7 * slot + rows] = jnp.where(low_r, third, 0.0)
        wbuf[rows : rows + 1] = high[head : head + 1]
        wbuf[rows + 1 : rows + 2] = middle[head : head + 1]
        wbuf[rows + 2 : rows + 3] = rest_[head : head + 1]
        pay[head, 5 * tokens :] = wbuf[...].astype(BF16)
    for copy in copy_all([(pay.at[chip ^ k], outs[k]) for k in range(heads)], sems):
        copy.wait()


def pack_queries(width, heads, q_ref, *rest):
    outs, (pay, sems) = rest[:heads], rest[heads:]
    chip, _ = chip_core(width)
    tokens = q_ref.shape[0]
    mid = tokens // 2
    low = low_lanes(mid)
    for head in range(heads):
        whole, half = tiles_of(head)
        pay[head, 0:tokens] = q_ref[:, whole : whole + LANES]
        pay[head, tokens : 2 * tokens] = q_ref[:, whole + LANES : whole + 2 * LANES]
        top = q_ref[0:mid, half : half + LANES].astype(F32)
        bottom = q_ref[mid:, half : half + LANES].astype(F32)
        if head % 2:
            top = turned(top)
        else:
            bottom = turned(bottom)
        pay[head, 2 * tokens :] = jnp.where(low, top, bottom).astype(BF16)
    for copy in copy_all([(pay.at[chip ^ k], outs[k]) for k in range(heads)], sems):
        copy.wait()


def key_side(width, heads, rows, slot, tokens, scale, *refs):
    count = heads * width
    ins = refs[: count]
    grad_ref, copy_ref, nat_ref = refs[count : count + 3]
    buf, wbuf, natural, gates, hidden, target, sems = refs[count + 3 :]
    chip, core = chip_core(width)
    pairs = []
    for other in range(width):
        for i, k in enumerate(FAR_FIRST):
            source = (chip ^ k) * width + (core ^ other)
            src = ins[other * heads + i]
            if other == 0:
                pairs.append((src, buf.at[source]))
            else:
                pairs.append((src.at[pl.ds(5 * tokens, 8 * slot)], buf.at[source, pl.ds(5 * tokens, 8 * slot)]))
    for copy in copy_all(pairs, sems):
        copy.wait()
    wide = 3 * LANES
    width_of = rows * count
    low = low_lanes(rows)
    for source in range(count):
        wbuf[...] = buf[source, 5 * tokens :].astype(F32)
        at = source * rows
        for m in range(2):
            for t in range(2):
                natural[at : at + rows, m * wide + t * LANES : m * wide + (t + 1) * LANES] = wbuf[
                    (2 * m + t) * slot : (2 * m + t) * slot + rows
                ]
        for t in range(2):
            natural[at : at + rows, 2 * wide + (t + 1) * LANES : 2 * wide + (t + 2) * LANES] = wbuf[
                (4 + t) * slot : (4 + t) * slot + rows
            ]
        both = wbuf[6 * slot : 6 * slot + rows]
        natural[at : at + rows, 2 * LANES : 3 * LANES] = jnp.where(low, both, 0.0)
        natural[at : at + rows, 2 * wide : 2 * wide + LANES] = jnp.where(low, 0.0, both)
        natural[at : at + rows, wide + 2 * LANES : wide + 3 * LANES] = wbuf[7 * slot : 7 * slot + rows]
    nat_ref[...] = natural[...].astype(BF16)
    odd = lax.rem(chip, 2)
    copy_ref[0 : 2 * LANES] = natural[pl.ds(pl.multiple_of(odd * HALF, HALF), 2 * LANES)].astype(BF16)
    copy_ref[2 * LANES : 2 * LANES + HALF] = natural[
        pl.ds(pl.multiple_of((1 - odd) * 2 * LANES, HALF), HALF)
    ].astype(BF16)
    copy_ref[width_of:] = jnp.zeros((copy_ref.shape[0] - width_of, copy_ref.shape[1]), BF16)

    steps = [
        jnp.sum(buf[j * width + core, 5 * tokens : 5 * tokens + slot].astype(F32)[rows : rows + 3], axis=0, keepdims=True)
        for j in range(heads)
    ]
    steps = jnp.concatenate(steps, axis=0).T
    w13 = copy_ref[:, 0 : 2 * wide]
    w2 = copy_ref[:, 2 * wide :]
    for j in range(heads):
        block = buf[j * width + core, 0 : 5 * tokens]
        keys = jnp.concatenate([block[0:tokens], block[tokens : 2 * tokens], block[2 * tokens : 3 * tokens]], axis=1)
        values = jnp.concatenate(
            [block[2 * tokens : 3 * tokens], block[3 * tokens : 4 * tokens], block[4 * tokens :]], axis=1
        )
        at = j * tokens
        tgt = (-steps[:, j : j + 1] * values.astype(F32)).astype(BF16)
        both = dot(keys, w13, ((1,), (0,))) * scale
        back = dot(tgt, w2, ((1,), (1,))) * scale
        gate, up = both[:, :wide], both[:, wide:]
        sig = 1.0 / (1.0 + jnp.exp(-gate))
        silu = gate * sig
        gates[at : at + tokens, 0:wide] = (back * up * (sig * (1.0 + gate * (1.0 - sig)))).astype(BF16)
        gates[at : at + tokens, wide:] = (back * silu).astype(BF16)
        hidden[at : at + tokens] = (silu * up).astype(BF16)
        target[at : at + tokens] = tgt
    all_keys = jnp.concatenate(
        [
            jnp.concatenate([buf[j * width + core, t * tokens : (t + 1) * tokens] for t in range(3)], axis=1)
            for j in range(heads)
        ],
        axis=0,
    )
    grads13 = dot(all_keys, gates[...], ((0,), (0,))) * scale
    grads2 = dot(hidden[...], target[...], ((0,), (0,))) * scale
    first_row = pl.multiple_of(odd * HALF, HALF)
    last_row = pl.multiple_of((1 - odd) * 2 * LANES, HALF)
    grad_ref[pl.ds(first_row, 2 * LANES), 0 : 2 * wide] = grads13[0 : 2 * LANES]
    grad_ref[pl.ds(last_row, HALF), 0 : 2 * wide] = grads13[2 * LANES : 2 * LANES + HALF]
    grad_ref[pl.ds(first_row, 2 * LANES), 2 * wide :] = grads2[0 : 2 * LANES]
    grad_ref[pl.ds(last_row, HALF), 2 * wide :] = grads2[2 * LANES : 2 * LANES + HALF]


def query_side(width, heads, tokens, scale, span, steps, *refs):
    count = heads * width
    half_heads = heads // 2
    kv = refs[:count]
    qs = refs[count : count + half_heads]
    copy_ref, fast_gain_ref, window_gain_ref = refs[count + half_heads : count + half_heads + 3]
    rest = refs[-(half_heads + 5) :]
    outs, (buf, qbuf, pay, sems, out_sems) = rest[:half_heads], rest[half_heads:]
    chip, core = chip_core(width)
    pairs = []
    for other in range(width):
        for i, k in enumerate(FAR_FIRST):
            source = (chip ^ k) * width + (core ^ other)
            pairs.append((kv[other * heads + i].at[pl.ds(0, 5 * tokens)], buf.at[source]))
    for i, k in enumerate(steps):
        pairs.append((qs[i], qbuf.at[lax.rem(chip ^ k, half_heads)]))
    for copy in copy_all(pairs, sems):
        copy.wait()
    wide = 3 * LANES
    mid = tokens // 2
    low = low_lanes(mid)
    high = jnp.logical_not(low_lanes(2 * tokens))
    size = heads * 40

    def query_block(j):
        tail = qbuf[j, 2 * tokens :].astype(F32)
        half = jnp.concatenate([jnp.where(low, tail, 0.0), jnp.where(low, turned(tail), 0.0)], axis=0)
        return jnp.concatenate([qbuf[j, 0:tokens], qbuf[j, tokens : 2 * tokens], half.astype(BF16)], axis=1)

    def two_blocks(j):
        place = j * width + core
        slot = j % half_heads
        q = jnp.concatenate([query_block(slot), query_block(slot + 1)], axis=0)
        blocks = min(width * (j + 2), span + 1 + width)
        start = 0 if blocks == width * (j + 2) else jnp.maximum(place - span, 0)
        keys_seen = blocks * tokens
        seen = buf[pl.ds(start, blocks)]
        tiles = [seen[:, t * tokens : (t + 1) * tokens].reshape(keys_seen, LANES) for t in range(5)]
        row = lax.broadcasted_iota(jnp.int32, (2 * tokens, 1), 0)
        row = jnp.where(row < tokens, row, row + (width - 1) * tokens) + (place - start) * tokens
        distance = row - lax.broadcasted_iota(jnp.int32, (2 * tokens, keys_seen), 1)
        allowed = distance >= 0
        if keys_seen > span * tokens:
            allowed = allowed & (distance < span * tokens)
        score = dot(q, jnp.concatenate(tiles[0:3], axis=1), ((1,), (1,)))
        score = jnp.where(allowed, score, -jnp.inf)
        top = jnp.max(score, axis=1, keepdims=True)
        weight = jnp.exp2((score - top) * (scale * math.log2(math.e)))
        total = jnp.sum(weight, axis=1, keepdims=True)
        attended = dot(weight.astype(BF16), jnp.concatenate(tiles[2:5], axis=1), ((1,), (0,))) / total
        attended = jnp.concatenate([jnp.where(high, attended[:, 0:LANES], 0.0), attended[:, LANES:]], axis=1)
        mean_sq = jnp.sum(attended * attended, axis=1, keepdims=True) * (1.0 / size)
        window_part = attended * lax.rsqrt(mean_sq + 1e-05) * window_gain_ref[...]

        both = dot(q, copy_ref[:, 0 : 2 * wide], ((1,), (0,))) * scale
        gate, up = both[:, :wide], both[:, wide:]
        hid = (gate / (1.0 + jnp.exp(-gate)) * up).astype(BF16)
        out = dot(hid, copy_ref[:, 2 * wide :], ((1,), (0,))) * scale
        mean_sq = jnp.sum(out * out, axis=1, keepdims=True) * (1.0 / size)
        layer = out * lax.rsqrt(mean_sq + 1e-05) * fast_gain_ref[...] + window_part
        for i in range(2):
            part = layer[i * tokens : (i + 1) * tokens]
            pay[slot + i, 0:tokens] = part[:, LANES : 2 * LANES].astype(BF16)
            pay[slot + i, tokens : 2 * tokens] = part[:, 2 * LANES :].astype(BF16)
            pay[slot + i, 2 * tokens :] = jnp.where(
                low, turned(part[mid:, 0:LANES]), part[0:mid, 0:LANES]
            ).astype(BF16)

    first_half = (chip ^ steps[0]) < half_heads

    @pl.when(first_half)
    def _():
        for j in range(0, half_heads, 2):
            two_blocks(j)

    @pl.when(jnp.logical_not(first_half))
    def _():
        for j in range(half_heads, heads, 2):
            two_blocks(j)

    out_pairs = [(pay.at[lax.rem(chip ^ k, half_heads)], outs[i]) for i, k in enumerate(steps)]
    for copy in copy_all(out_pairs, out_sems):
        copy.wait()


def pack_momentum(width, heads, rows, slot, mine_ref, *refs):
    others = refs[: width - 1]
    nat_ref = refs[width - 1]
    outs = refs[width : width + heads]
    total, scales, pieces, wbuf, pay, sems = refs[width + heads :]
    chip, core = chip_core(width)
    summed = mine_ref[...]
    for other in others:
        summed = summed + other[...]
    summed = summed.astype(BF16).astype(F32)
    total[...] = summed
    old = nat_ref[...].astype(F32)
    moved = old - summed
    ratio = (jnp.sum(old * old, axis=0, keepdims=True) + 1e-06) / (jnp.sum(moved * moved, axis=0, keepdims=True) + 1e-06)
    ratio = jnp.sqrt(ratio)
    high = ratio.astype(BF16).astype(F32)
    scales[0:1] = high
    scales[1:2] = ratio - high
    wide = 3 * LANES
    low = low_lanes(rows)
    low_1 = low_lanes(2)
    for source in range(heads * width):
        pieces[source, 0:rows] = total[source * rows : (source + 1) * rows]
    wbuf[...] = jnp.zeros_like(wbuf)
    for head in range(heads):
        source = head * width + core
        for m in range(3):
            for t in range(2):
                lane = m * wide + t * LANES + (LANES if m == 2 else 0)
                at = (2 * m + t) * slot
                wbuf[at : at + rows] = pieces[source, 0:rows, lane : lane + LANES]
                wbuf[at + rows : at + rows + 2] = scales[0:2, lane : lane + LANES]
        at = 6 * slot
        wbuf[at : at + rows] = jnp.where(
            low, pieces[source, 0:rows, 2 * LANES : 3 * LANES], pieces[source, 0:rows, 2 * wide : 2 * wide + LANES]
        )
        wbuf[at + rows : at + rows + 2] = jnp.where(
            low_1, scales[0:2, 2 * LANES : 3 * LANES], scales[0:2, 2 * wide : 2 * wide + LANES]
        )
        at = 7 * slot
        wbuf[at : at + rows] = pieces[source, 0:rows, wide + 2 * LANES : wide + 3 * LANES]
        wbuf[at + rows : at + rows + 2] = scales[0:2, wide + 2 * LANES : wide + 3 * LANES]
        pay[head] = wbuf[...].astype(BF16)
    for copy in copy_all([(pay.at[chip ^ k], outs[k]) for k in range(heads)], sems):
        copy.wait()


def unpack_layer(width, heads, tokens, *refs):
    layers = refs[:heads]
    layer_ref, lbuf, sems = refs[heads:]
    chip, _ = chip_core(width)
    for copy in copy_all([(layers[i], lbuf.at[chip ^ k]) for i, k in enumerate(FAR_FIRST)], sems):
        copy.wait()
    mid = tokens // 2
    low = low_lanes(mid)
    for head in range(heads):
        whole, half = tiles_of(head)
        layer_ref[:, whole : whole + LANES] = lbuf[head, 0:tokens]
        layer_ref[:, whole + LANES : whole + 2 * LANES] = lbuf[head, tokens : 2 * tokens]
    for head in range(0, heads, 2):
        _, half = tiles_of(head)
        even = lbuf[head, 2 * tokens :].astype(F32)
        odd = lbuf[head + 1, 2 * tokens :].astype(F32)
        layer_ref[0:mid, half : half + LANES] = jnp.where(low, turned(even), odd).astype(BF16)
        layer_ref[mid:, half : half + LANES] = jnp.where(low, even, turned(odd)).astype(BF16)


def unpack_moments(width, heads, rows, slot, *refs):
    moments = refs[:heads]
    fw_ref, new_ref, momentum_ref, mbuf, wbuf, sems = refs[heads:]
    chip, _ = chip_core(width)
    for copy in copy_all([(moments[i], mbuf.at[chip ^ k]) for i, k in enumerate(FAR_FIRST)], sems):
        copy.wait()
    low_r = low_lanes(slot)
    matrix = fw_ref.shape[1] // 3

    def write(lane, block):
        moment = block[0:rows]
        factor = block[rows : rows + 1] + block[rows + 1 : rows + 2]
        momentum_ref[:, lane : lane + LANES] = moment
        new_ref[:, lane : lane + LANES] = (fw_ref[:, lane : lane + LANES] - moment) * factor

    for head in range(heads):
        whole, half = tiles_of(head)
        wbuf[head] = mbuf[head].astype(F32)
        for m in range(3):
            for t in range(2):
                write(m * matrix + whole + t * LANES, wbuf[head, (2 * m + t) * slot : (2 * m + t + 1) * slot])
    for head in range(0, heads, 2):
        _, half = tiles_of(head)
        even = wbuf[head, 6 * slot : 7 * slot]
        odd = wbuf[head + 1, 6 * slot : 7 * slot]
        write(half, jnp.where(low_r, even, turned(odd)))
        write(2 * matrix + half, jnp.where(low_r, turned(even), odd))
        even = wbuf[head, 7 * slot :]
        odd = wbuf[head + 1, 7 * slot :]
        write(matrix + half, jnp.where(low_r, even, turned(odd)))


def shards(queries, key_vectors, value_vectors, step_sizes, fast_weights, fast_gain, window_gain):
    tokens = queries.shape[0]
    heads = step_sizes.shape[1]
    head_width = queries.shape[1] // heads
    scale = 1.0 / math.sqrt(head_width)
    count = lax.axis_size("seq")
    width = count // heads
    rows = fast_weights.shape[0]
    slot = -(-(rows + 3) // 8) * 8
    span = WINDOW // tokens
    wide = 3 * LANES
    params = pltpu.CompilerParams(vmem_limit_bytes=VMEM_LIMIT)
    sem = pltpu.SemaphoreType.DMA
    key_rows = 5 * tokens + 8 * slot
    query_rows = 2 * tokens + tokens // 2

    def cost(micros):
        return pl.CostEstimate(flops=micros * 500_000_000, transcendentals=0, bytes_accessed=micros * 2_000_000)

    def across(value, step):
        return lax.ppermute(value, "seq", [(i, i ^ step) for i in range(count)])

    def exchange(pieces):
        return [across(pieces[k], k * width) if k else pieces[0] for k in FAR_FIRST]

    def packed(size):
        return [jax.ShapeDtypeStruct((size, LANES), BF16)] * heads

    key_pieces = pl.pallas_call(
        functools.partial(pack_keys, width, heads, rows, slot),
        out_shape=packed(key_rows),
        in_specs=[VMEM] * 4,
        out_specs=[ANY] * heads,
        scratch_shapes=[
            pltpu.VMEM((heads, key_rows, LANES), BF16),
            pltpu.VMEM((8 * slot, LANES), F32),
            sem((heads,)),
        ],
        compiler_params=params,
        cost_estimate=cost(3),
        name="pack_keys",
    )(key_vectors, value_vectors, step_sizes.T, fast_weights)
    query_pieces = pl.pallas_call(
        functools.partial(pack_queries, width, heads),
        out_shape=packed(query_rows),
        in_specs=[VMEM],
        out_specs=[ANY] * heads,
        scratch_shapes=[pltpu.VMEM((heads, query_rows, LANES), BF16), sem((heads,))],
        compiler_params=params,
        cost_estimate=cost(1),
        name="pack_queries",
    )(queries)
    key_blocks = exchange(key_pieces)
    for other in range(1, width):
        key_blocks = key_blocks + [across(key_blocks[k], other) for k in range(heads)]
    query_blocks = exchange(query_pieces)

    gradient, copies, natural = pl.pallas_call(
        functools.partial(key_side, width, heads, rows, slot, tokens, scale),
        out_shape=[
            jax.ShapeDtypeStruct((head_width, 3 * wide), F32),
            jax.ShapeDtypeStruct((wide, 3 * wide), BF16),
            jax.ShapeDtypeStruct((head_width, 3 * wide), BF16),
        ],
        in_specs=[ANY] * count,
        out_specs=[VMEM] * 3,
        scratch_shapes=[
            pltpu.VMEM((count, key_rows, LANES), BF16),
            pltpu.VMEM((8 * slot, LANES), F32),
            pltpu.VMEM((head_width, 3 * wide), F32),
            pltpu.VMEM((heads * tokens, 2 * wide), BF16),
            pltpu.VMEM((heads * tokens, wide), BF16),
            pltpu.VMEM((heads * tokens, wide), BF16),
            sem((count,)),
        ],
        compiler_params=params,
        cost_estimate=cost(8),
        name="key_side",
    )(*key_blocks)
    gradients = [across(gradient, other) for other in range(1, width)]

    head = lax.axis_index("seq") // width
    odd = head % 2

    def gain_row(gain):
        row = lax.dynamic_slice_in_dim(gain.reshape(heads, head_width), head, 1, 0)
        gap = jnp.zeros((1, HALF), F32)
        even_row = jnp.concatenate([gap, row[:, 2 * LANES :], row[:, : 2 * LANES]], axis=1)
        odd_row = jnp.concatenate([gap, row], axis=1)
        return jnp.where(odd == 1, odd_row, even_row)

    momentum_pieces = pl.pallas_call(
        functools.partial(pack_momentum, width, heads, rows, slot),
        out_shape=packed(8 * slot),
        in_specs=[VMEM] * (width + 1),
        out_specs=[ANY] * heads,
        scratch_shapes=[
            pltpu.VMEM((head_width, 3 * wide), F32),
            pltpu.VMEM((8, 3 * wide), F32),
            pltpu.VMEM((count, slot, 3 * wide), F32),
            pltpu.VMEM((8 * slot, LANES), F32),
            pltpu.VMEM((heads, 8 * slot, LANES), BF16),
            sem((heads,)),
        ],
        compiler_params=params,
        cost_estimate=cost(2),
        name="pack_momentum",
    )(gradient, *gradients, natural)
    moments = exchange(momentum_pieces)

    half_heads = heads // 2
    gains = (gain_row(fast_gain), gain_row(window_gain))

    def query_half(steps, blocks, *after):
        return pl.pallas_call(
            functools.partial(query_side, width, heads, tokens, scale, span, steps),
            out_shape=packed(query_rows)[:half_heads],
            in_specs=[ANY] * (count + half_heads) + [VMEM] * 3 + [ANY] * len(after),
            out_specs=[ANY] * half_heads,
            scratch_shapes=[
                pltpu.VMEM((count, 5 * tokens, LANES), BF16),
                pltpu.VMEM((half_heads, query_rows, LANES), BF16),
                pltpu.VMEM((half_heads, query_rows, LANES), BF16),
                sem((count + half_heads,)),
                sem((half_heads,)),
            ],
            compiler_params=params,
            cost_estimate=cost(40),
            name="query_side",
        )(*key_blocks, *blocks, copies, *gains, *after)

    far, near = FAR_FIRST[:half_heads], FAR_FIRST[half_heads:]
    layers = query_half(far, query_blocks[:half_heads])
    layers = layers + query_half(near, query_blocks[half_heads:], momentum_pieces[0])
    layers = [across(piece, k * width) if k else piece for piece, k in zip(layers, FAR_FIRST)]

    new_weights, momentum = pl.pallas_call(
        functools.partial(unpack_moments, width, heads, rows, slot),
        out_shape=[jax.ShapeDtypeStruct(fast_weights.shape, F32)] * 2,
        in_specs=[ANY] * heads + [VMEM],
        out_specs=[VMEM] * 2,
        scratch_shapes=[
            pltpu.VMEM((heads, 8 * slot, LANES), BF16),
            pltpu.VMEM((heads, 8 * slot, LANES), F32),
            sem((heads,)),
        ],
        compiler_params=params,
        cost_estimate=cost(3),
        name="unpack_moments",
    )(*moments, fast_weights)
    layer_out = pl.pallas_call(
        functools.partial(unpack_layer, width, heads, tokens),
        out_shape=jax.ShapeDtypeStruct(queries.shape, BF16),
        in_specs=[ANY] * heads,
        out_specs=VMEM,
        scratch_shapes=[pltpu.VMEM((heads, query_rows, LANES), BF16), sem((heads,))],
        compiler_params=params,
        cost_estimate=cost(2),
        name="unpack_layer",
    )(*layers)
    return (layer_out, new_weights, momentum)


def solution(mesh):
    in_specs = (
        P(("groups", "seq"), None),
        P(("groups", "seq"), None),
        P(("groups", "seq"), None),
        P(("groups", "seq"), None),
        P("seq", None),
        P(),
        P(),
    )
    out_specs = (P(("groups", "seq"), None), P(("groups", "seq"), None), P(("groups", "seq"), None))
    return jax.shard_map(shards, mesh=mesh, in_specs=in_specs, out_specs=out_specs, check_vma=False)
```

```python
import functools
import math

import jax
import jax.numpy as jnp
from jax import lax
from jax.experimental import pallas as pl
from jax.experimental.pallas import tpu as pltpu
from jax.sharding import PartitionSpec as P

WINDOW = 1024
LANES = 128
HALF = 64
VMEM_LIMIT = 24 * 1024 * 1024
BF16 = jnp.bfloat16
F32 = jnp.float32
I32 = jnp.int32
FAR = (4, 5, 6, 7)
NEAR = (2, 3, 1, 0)
HBM = pl.BlockSpec(memory_space=pltpu.HBM)
ANY = pl.BlockSpec(memory_space=pl.ANY)
VMEM = pl.BlockSpec(memory_space=pltpu.VMEM)


def tiles_of(head):
    first = (5 * head) // 2
    odd = head % 2
    return (first + odd) * LANES, (first if odd else first + 2) * LANES


def turned(tile):
    return pltpu.roll(tile, HALF, axis=1)


def low_lanes(rows):
    return lax.broadcasted_iota(I32, (rows, LANES), 1) < HALF


def dot(left, right, contract):
    return lax.dot_general(left, right, (contract, ((), ())), preferred_element_type=F32)


def chip_core(width):
    place = lax.axis_index("seq")
    return place // width, lax.rem(place, width)


def slot_of(index, slot):
    part = (index * (65536 // slot + (65536 % slot > 0))) >> 16
    return part, index - part * slot


def natural_row(row, odd):
    return jnp.where(odd == 1, jnp.where(row < 2 * LANES, row + HALF, row - 2 * LANES), row)


def copy_all(pairs, sems):
    copies = [pltpu.make_async_copy(src, dst, sems.at[i]) for i, (src, dst) in enumerate(pairs)]
    for copy in copies:
        copy.start()
    return copies


def pack_keys(width, heads, rows, slot, steps, k_hbm, v_hbm, step_ref, fw_hbm, *rest):
    few = heads // 2
    outs, (k_ref, v_ref, fw_ref, pay, wbuf, sems) = rest[:few], rest[few:]
    chip, _ = chip_core(width)
    side = (chip ^ steps[0]) // few
    slab = k_ref.shape[1]
    matrix = fw_hbm.shape[1] // 3
    at = pl.multiple_of(side * slab, LANES)
    pairs = [(k_hbm.at[:, pl.ds(at, slab)], k_ref), (v_hbm.at[:, pl.ds(at, slab)], v_ref)]
    for m in range(3):
        lane = pl.multiple_of(side * slab + m * matrix, LANES)
        pairs.append((fw_hbm.at[:, pl.ds(lane, slab)], fw_ref.at[m]))
    copies = copy_all(pairs, sems)
    tokens = k_ref.shape[0]
    low = low_lanes(tokens)
    low_r = low_lanes(rows)
    for copy in copies:
        copy.wait()
    wbuf[...] = jnp.zeros_like(wbuf)
    for head in range(few):
        whole, half = tiles_of(head)
        odd = head % 2
        pay[head, 0:tokens] = k_ref[:, whole : whole + LANES]
        pay[head, tokens : 2 * tokens] = k_ref[:, whole + LANES : whole + 2 * LANES]
        pay[head, 3 * tokens : 4 * tokens] = v_ref[:, whole : whole + LANES]
        pay[head, 4 * tokens : 5 * tokens] = v_ref[:, whole + LANES : whole + 2 * LANES]
        k_half = k_ref[:, half : half + LANES].astype(F32)
        v_half = v_ref[:, half : half + LANES].astype(F32)
        mixed = jnp.where(low, turned(k_half) if odd else k_half, v_half if odd else turned(v_half))
        pay[head, 2 * tokens : 3 * tokens] = mixed.astype(BF16)
        halves = []
        for m in range(3):
            for t in range(2):
                spot = (2 * m + t) * slot
                wbuf[head, spot : spot + rows] = fw_ref[m, :, whole + t * LANES : whole + (t + 1) * LANES]
            halves.append(fw_ref[m, :, half : half + LANES])
        first, third, second = halves
        if odd:
            first, third = turned(first), turned(third)
        else:
            second = turned(second)
        wbuf[head, 6 * slot : 6 * slot + rows] = jnp.where(low_r, first, second)
        wbuf[head, 7 * slot : 7 * slot + rows] = jnp.where(low_r, third, 0.0)
        step = step_ref[pl.ds(side * few + head, 1)]
        high = step.astype(BF16).astype(F32)
        middle = (step - high).astype(BF16).astype(F32)
        wbuf[head, rows : rows + 1] = high
        wbuf[head, rows + 1 : rows + 2] = middle
        wbuf[head, rows + 2 : rows + 3] = step - high - middle
        pay[head, 5 * tokens :] = wbuf[head].astype(BF16)
    for i, k in enumerate(steps):
        outs[i][...] = pay[lax.rem(chip ^ k, few)]


def pack_queries(width, heads, q_ref, *rest):
    outs, (pay,) = rest[:heads], rest[heads:]
    chip, _ = chip_core(width)
    tokens = q_ref.shape[0]
    mid = tokens // 2
    low = low_lanes(mid)
    for head in range(heads):
        whole, half = tiles_of(head)
        pay[head, 0:tokens] = q_ref[:, whole : whole + LANES]
        pay[head, tokens : 2 * tokens] = q_ref[:, whole + LANES : whole + 2 * LANES]
        top = q_ref[0:mid, half : half + LANES].astype(F32)
        bottom = q_ref[mid:, half : half + LANES].astype(F32)
        if head % 2:
            top = turned(top)
        else:
            bottom = turned(bottom)
        pay[head, 2 * tokens :] = jnp.where(low, top, bottom).astype(BF16)
    for i, k in enumerate(FAR + NEAR):
        outs[i][...] = pay[chip ^ k]


def key_side(width, heads, rows, slot, tokens, scale, *refs):
    count = heads * width
    ins = refs[:count]
    grad_ref, copy_ref, kv_ref = refs[count : count + 3]
    gates, hidden, target = refs[count + 3 :]
    chip, core = chip_core(width)
    odd = lax.rem(chip, 2)
    wide = 3 * LANES
    size = rows * count
    place = {k: i for i, k in enumerate(FAR + NEAR)}
    blocks = [ins[other * heads + place[k]] for other in range(width) for k in range(heads)]
    for index, block in enumerate(blocks):
        other, k = divmod(index, heads)
        kv_ref[(chip ^ k) * width + (core ^ other)] = block[0 : 5 * tokens]
    parts = [block[5 * tokens :].astype(F32) for block in blocks]
    column, row_in = slot_of(lax.broadcasted_iota(I32, (wide, count * slot), 1), slot)
    source = ((column & (heads - 1)) ^ chip) * width + (core ^ (column >> (heads.bit_length() - 1)))
    wanted = lax.broadcasted_iota(I32, (wide, count * slot), 0)
    chosen = (source * rows + row_in == natural_row(wanted, odd)) & (row_in < rows) & (wanted < size)
    chosen = jnp.where(chosen, 1.0, 0.0).astype(BF16)
    gathered = [
        jnp.concatenate([part[t * slot : (t + 1) * slot] for part in parts], axis=0).astype(BF16) for t in range(8)
    ]
    placed = dot(chosen, jnp.concatenate(gathered, axis=1), ((1,), (0,)))
    tile = [placed[:, t * LANES : (t + 1) * LANES] for t in range(8)]
    low = low_lanes(wide)
    columns = [tile[0], tile[1], jnp.where(low, tile[6], 0.0), tile[2], tile[3], tile[7]]
    columns += [jnp.where(low, 0.0, tile[6]), tile[4], tile[5]]
    for t, column_tile in enumerate(columns):
        copy_ref[:, t * LANES : (t + 1) * LANES] = column_tile.astype(BF16)

    steps = [jnp.sum(part[rows : rows + 3], axis=0, keepdims=True) for part in parts[:heads]]
    steps = jnp.concatenate(steps, axis=0).T
    w13 = copy_ref[:, 0 : 2 * wide]
    w2 = copy_ref[:, 2 * wide :]
    for j in range(heads):
        block = blocks[j]
        keys = jnp.concatenate([block[t * tokens : (t + 1) * tokens] for t in range(3)], axis=1)
        values = jnp.concatenate([block[t * tokens : (t + 1) * tokens] for t in range(2, 5)], axis=1)
        at = j * tokens
        tgt = (-steps[:, j : j + 1] * values.astype(F32)).astype(BF16)
        both = dot(keys, w13, ((1,), (0,))) * scale
        back = dot(tgt, w2, ((1,), (1,))) * scale
        gate, up = both[:, :wide], both[:, wide:]
        sig = 1.0 / (1.0 + jnp.exp(-gate))
        silu = gate * sig
        gates[at : at + tokens, 0:wide] = (back * up * (sig * (1.0 + gate * (1.0 - sig)))).astype(BF16)
        gates[at : at + tokens, wide:] = (back * silu).astype(BF16)
        hidden[at : at + tokens] = (silu * up).astype(BF16)
        target[at : at + tokens] = tgt
    all_keys = [
        jnp.concatenate([blocks[j][t * tokens : (t + 1) * tokens] for t in range(3)], axis=1) for j in range(heads)
    ]
    grads13 = dot(jnp.concatenate(all_keys, axis=0), gates[...], ((0,), (0,))) * scale
    grads2 = dot(hidden[...], target[...], ((0,), (0,))) * scale
    grad_ref[:, 0 : 2 * wide] = grads13[0:size]
    grad_ref[:, 2 * wide :] = grads2[0:size]


def query_side(width, heads, tokens, scale, span, steps, *refs):
    few = heads // 2
    kv_ref, copy_ref, fast_gain_ref, window_gain_ref = refs[:4]
    qs = refs[4 : 4 + few]
    outs, (qbuf, pay) = refs[-(few + 2) : -2], refs[-2:]
    chip, core = chip_core(width)
    for i, k in enumerate(steps):
        qbuf[lax.rem(chip ^ k, few)] = qs[i][...]
    wide = 3 * LANES
    mid = tokens // 2
    low = low_lanes(mid)
    high = jnp.logical_not(low_lanes(2 * tokens))
    size = heads * 40

    def query_block(j):
        tail = qbuf[j, 2 * tokens :].astype(F32)
        half = jnp.concatenate([jnp.where(low, tail, 0.0), jnp.where(low, turned(tail), 0.0)], axis=0)
        return jnp.concatenate([qbuf[j, 0:tokens], qbuf[j, tokens : 2 * tokens], half.astype(BF16)], axis=1)

    def two_blocks(j):
        place = j * width + core
        slot = j % few
        q = jnp.concatenate([query_block(slot), query_block(slot + 1)], axis=0)
        blocks = min(width * (j + 2), span + 1 + width)
        start = 0 if blocks == width * (j + 2) else jnp.maximum(place - span, 0)
        keys_seen = blocks * tokens
        seen = kv_ref[pl.ds(start, blocks)]
        tiles = [seen[:, t * tokens : (t + 1) * tokens].reshape(keys_seen, LANES) for t in range(5)]
        row = lax.broadcasted_iota(I32, (2 * tokens, 1), 0)
        row = jnp.where(row < tokens, row, row + (width - 1) * tokens) + (place - start) * tokens
        distance = row - lax.broadcasted_iota(I32, (2 * tokens, keys_seen), 1)
        allowed = distance >= 0
        if keys_seen > span * tokens:
            allowed = allowed & (distance < span * tokens)
        score = dot(q, jnp.concatenate(tiles[0:3], axis=1), ((1,), (1,)))
        score = jnp.where(allowed, score, -jnp.inf)
        top = jnp.max(score, axis=1, keepdims=True)
        weight = jnp.exp2((score - top) * (scale * math.log2(math.e)))
        total = jnp.sum(weight, axis=1, keepdims=True)
        attended = dot(weight.astype(BF16), jnp.concatenate(tiles[2:5], axis=1), ((1,), (0,))) / total
        attended = jnp.concatenate([jnp.where(high, attended[:, 0:LANES], 0.0), attended[:, LANES:]], axis=1)
        mean_sq = jnp.sum(attended * attended, axis=1, keepdims=True) * (1.0 / size)
        window_part = attended * lax.rsqrt(mean_sq + 1e-05) * window_gain_ref[...]

        both = dot(q, copy_ref[:, 0 : 2 * wide], ((1,), (0,))) * scale
        gate, up = both[:, :wide], both[:, wide:]
        hid = (gate / (1.0 + jnp.exp(-gate)) * up).astype(BF16)
        out = dot(hid, copy_ref[:, 2 * wide :], ((1,), (0,))) * scale
        mean_sq = jnp.sum(out * out, axis=1, keepdims=True) * (1.0 / size)
        layer = out * lax.rsqrt(mean_sq + 1e-05) * fast_gain_ref[...] + window_part
        for i in range(2):
            part = layer[i * tokens : (i + 1) * tokens]
            pay[slot + i, 0:tokens] = part[:, LANES : 2 * LANES].astype(BF16)
            pay[slot + i, tokens : 2 * tokens] = part[:, 2 * LANES :].astype(BF16)
            pay[slot + i, 2 * tokens :] = jnp.where(
                low, turned(part[mid:, 0:LANES]), part[0:mid, 0:LANES]
            ).astype(BF16)

    first_half = (chip ^ steps[0]) < few

    @pl.when(first_half)
    def _():
        for j in range(0, few, 2):
            two_blocks(j)

    @pl.when(jnp.logical_not(first_half))
    def _():
        for j in range(few, heads, 2):
            two_blocks(j)

    for i, k in enumerate(steps):
        outs[i][...] = pay[lax.rem(chip ^ k, few)]


def pack_momentum(width, heads, rows, slot, *refs):
    grads = refs[:width]
    copy_ref = refs[width]
    layers = refs[width + 1 : width + 1 + heads]
    outs = refs[width + 1 + heads : width + 1 + 2 * heads]
    (pay,) = refs[width + 1 + 2 * heads :]
    chip, core = chip_core(width)
    odd = lax.rem(chip, 2)
    size = rows * heads * width
    wide = 3 * LANES
    summed = grads[0][...]
    for other in grads[1:]:
        summed = summed + other[...]
    rounded = summed.astype(BF16)
    old = copy_ref[0:size].astype(F32)
    moved = old - rounded.astype(F32)
    ratio = (jnp.sum(old * old, axis=0, keepdims=True) + 1e-06) / (jnp.sum(moved * moved, axis=0, keepdims=True) + 1e-06)
    ratio = jnp.sqrt(ratio)
    ratio_high = ratio.astype(BF16).astype(F32)
    head, row_in = slot_of(lax.broadcasted_iota(I32, (heads * slot, size), 0), slot)
    wanted = (head * width + core) * rows + row_in
    chosen = (wanted == natural_row(lax.broadcasted_iota(I32, (heads * slot, size), 1), odd)) & (row_in < rows)
    picked = dot(jnp.where(chosen, 1.0, 0.0).astype(BF16), rounded, ((1,), (0,)))
    _, row_in = slot_of(lax.broadcasted_iota(I32, (heads * slot, 1), 0), slot)
    picked = jnp.where(row_in == rows, ratio_high, jnp.where(row_in == rows + 1, ratio - ratio_high, picked))
    tile = [picked[:, t * LANES : (t + 1) * LANES] for t in range(9)]
    low = low_lanes(heads * slot)
    order = [tile[0], tile[1], tile[3], tile[4], tile[7], tile[8], jnp.where(low, tile[2], tile[6]), tile[5]]
    for b in range(heads):
        pay[b] = jnp.concatenate([part[b * slot : (b + 1) * slot] for part in order], axis=0).astype(BF16)
    for i, k in enumerate(FAR + NEAR):
        cut = layers[i].shape[0]
        outs[i][0:cut] = layers[i][...]
        outs[i][cut:] = pay[chip ^ k]


def unpack(width, heads, rows, slot, tokens, steps, *refs):
    few = heads // 2
    pieces = refs[:few]
    fw_hbm = refs[few]
    layer_hbm, new_hbm, momentum_hbm, buf, fw_ref, layer_ref, new_ref, momentum_ref, in_sems, sems = refs[-10:]
    chip, _ = chip_core(width)
    side = (chip ^ steps[0]) // few
    slab = layer_ref.shape[1]
    matrix = fw_hbm.shape[1] // 3

    def lanes(m):
        return pl.ds(pl.multiple_of(side * slab + m * matrix, LANES), slab)

    reads = copy_all([(fw_hbm.at[:, lanes(m)], fw_ref.at[m]) for m in range(3)], in_sems)
    for i, k in enumerate(steps):
        buf[lax.rem(chip ^ k, few)] = pieces[i][...]
    mid = tokens // 2
    cut = 2 * tokens + mid
    low = low_lanes(mid)
    low_r = low_lanes(slot)
    for head in range(few):
        whole, half = tiles_of(head)
        layer_ref[:, whole : whole + LANES] = buf[head, 0:tokens]
        layer_ref[:, whole + LANES : whole + 2 * LANES] = buf[head, tokens : 2 * tokens]
    for head in range(0, few, 2):
        _, half = tiles_of(head)
        even = buf[head, 2 * tokens : cut].astype(F32)
        odd = buf[head + 1, 2 * tokens : cut].astype(F32)
        layer_ref[0:mid, half : half + LANES] = jnp.where(low, turned(even), odd).astype(BF16)
        layer_ref[mid:, half : half + LANES] = jnp.where(low, even, turned(odd)).astype(BF16)
    writes = copy_all([(layer_ref, layer_hbm.at[:, lanes(0)])], sems)

    for copy in reads:
        copy.wait()

    def write(m, lane, block):
        moment = block[0:rows]
        factor = block[rows : rows + 1] + block[rows + 1 : rows + 2]
        momentum_ref[m, :, lane : lane + LANES] = moment
        new_ref[m, :, lane : lane + LANES] = (fw_ref[m, :, lane : lane + LANES] - moment) * factor

    moments = [buf[head, cut:].astype(F32) for head in range(few)]
    for head in range(few):
        whole, half = tiles_of(head)
        for m in range(3):
            for t in range(2):
                write(m, whole + t * LANES, moments[head][(2 * m + t) * slot : (2 * m + t + 1) * slot])
    for head in range(0, few, 2):
        _, half = tiles_of(head)
        even = moments[head][6 * slot : 7 * slot]
        odd = moments[head + 1][6 * slot : 7 * slot]
        write(0, half, jnp.where(low_r, even, turned(odd)))
        write(2, half, jnp.where(low_r, turned(even), odd))
        even = moments[head][7 * slot :]
        odd = moments[head + 1][7 * slot :]
        write(1, half, jnp.where(low_r, even, turned(odd)))
    pairs = [(new_ref.at[m], new_hbm.at[:, lanes(m)]) for m in range(3)]
    pairs += [(momentum_ref.at[m], momentum_hbm.at[:, lanes(m)]) for m in range(3)]
    for copy in writes + copy_all(pairs, sems.at[pl.ds(1, 6)]):
        copy.wait()


def shards(queries, key_vectors, value_vectors, step_sizes, fast_weights, fast_gain, window_gain):
    tokens = queries.shape[0]
    heads = step_sizes.shape[1]
    few = heads // 2
    head_width = queries.shape[1] // heads
    scale = 1.0 / math.sqrt(head_width)
    count = lax.axis_size("seq")
    width = count // heads
    rows = fast_weights.shape[0]
    slot = -(-(rows + 3) // 8) * 8
    span = WINDOW // tokens
    wide = 3 * LANES
    slab = few * head_width
    params = pltpu.CompilerParams(vmem_limit_bytes=VMEM_LIMIT)
    sem = pltpu.SemaphoreType.DMA
    key_rows = 5 * tokens + 8 * slot
    query_rows = 2 * tokens + tokens // 2
    out_rows = query_rows + 8 * slot

    def across(value, step):
        return lax.ppermute(value, "seq", [(i, i ^ step) for i in range(count)])

    def exchange(pieces, steps):
        return [across(piece, k * width) if k else piece for piece, k in zip(pieces, steps)]

    def packed(size, many):
        return [jax.ShapeDtypeStruct((size, LANES), BF16)] * many

    def cost(micros):
        return pl.CostEstimate(flops=micros * 500_000_000, transcendentals=0, bytes_accessed=micros * 2_000_000)

    def call(body, name, micros, *operands, **kwargs):
        return pl.pallas_call(
            body, compiler_params=params, cost_estimate=cost(micros), name=name, **kwargs
        )(*operands)

    step_rows = step_sizes.T

    def keys_for(steps):
        return call(
            functools.partial(pack_keys, width, heads, rows, slot, steps),
            "pack_keys",
            2,
            key_vectors,
            value_vectors,
            step_rows,
            fast_weights,
            out_shape=packed(key_rows, few),
            in_specs=[HBM, HBM, VMEM, HBM],
            out_specs=[VMEM] * few,
            scratch_shapes=[
                pltpu.VMEM((tokens, slab), BF16),
                pltpu.VMEM((tokens, slab), BF16),
                pltpu.VMEM((3, rows, slab), F32),
                pltpu.VMEM((few, key_rows, LANES), BF16),
                pltpu.VMEM((few, 8 * slot, LANES), F32),
                sem((5,)),
            ],
        )

    key_blocks = exchange(keys_for(FAR), FAR) + exchange(keys_for(NEAR), NEAR)
    for other in range(1, width):
        key_blocks = key_blocks + [across(block, other) for block in key_blocks[:heads]]
    query_pieces = call(
        functools.partial(pack_queries, width, heads),
        "pack_queries",
        1,
        queries,
        out_shape=packed(query_rows, heads),
        in_specs=[VMEM],
        out_specs=[VMEM] * heads,
        scratch_shapes=[pltpu.VMEM((heads, query_rows, LANES), BF16)],
    )
    query_blocks = exchange(query_pieces, FAR + NEAR)

    gradient, copies, key_values = call(
        functools.partial(key_side, width, heads, rows, slot, tokens, scale),
        "key_side",
        0,
        *key_blocks,
        out_shape=[
            jax.ShapeDtypeStruct((head_width, 3 * wide), F32),
            jax.ShapeDtypeStruct((wide, 3 * wide), BF16),
            jax.ShapeDtypeStruct((count, 5 * tokens, LANES), BF16),
        ],
        in_specs=[VMEM] * count,
        out_specs=[VMEM] * 3,
        scratch_shapes=[
            pltpu.VMEM((heads * tokens, 2 * wide), BF16),
            pltpu.VMEM((heads * tokens, wide), BF16),
            pltpu.VMEM((heads * tokens, wide), BF16),
        ],
    )
    gradients = [across(gradient, other) for other in range(1, width)]

    head = lax.axis_index("seq") // width
    odd = head % 2

    def gain_row(gain):
        row = lax.dynamic_slice_in_dim(gain.reshape(heads, head_width), head, 1, 0)
        gap = jnp.zeros((1, HALF), F32)
        even_row = jnp.concatenate([gap, row[:, 2 * LANES :], row[:, : 2 * LANES]], axis=1)
        odd_row = jnp.concatenate([gap, row], axis=1)
        return jnp.where(odd == 1, odd_row, even_row)

    gains = (gain_row(fast_gain), gain_row(window_gain))

    def layers_of(steps, blocks, micros):
        return call(
            functools.partial(query_side, width, heads, tokens, scale, span, steps),
            "query_side",
            micros,
            key_values,
            copies,
            *gains,
            *blocks,
            out_shape=packed(query_rows, few),
            in_specs=[VMEM] * (4 + few),
            out_specs=[VMEM] * few,
            scratch_shapes=[
                pltpu.VMEM((few, query_rows, LANES), BF16),
                pltpu.VMEM((few, query_rows, LANES), BF16),
            ],
        )

    near_layers = layers_of(NEAR, query_blocks[few:], 0)
    far_layers = layers_of(FAR, query_blocks[:few], 40)
    pieces = call(
        functools.partial(pack_momentum, width, heads, rows, slot),
        "pack_momentum",
        2,
        gradient,
        *gradients,
        copies,
        *far_layers,
        *near_layers,
        out_shape=packed(out_rows, heads),
        in_specs=[VMEM] * (width + 1 + heads),
        out_specs=[VMEM] * heads,
        scratch_shapes=[pltpu.VMEM((heads, 8 * slot, LANES), BF16)],
    )
    pieces = exchange(pieces, FAR + NEAR)

    def outputs_of(steps, blocks, *before):
        return call(
            functools.partial(unpack, width, heads, rows, slot, tokens, steps),
            "unpack",
            2,
            *blocks,
            fast_weights,
            *before,
            out_shape=[
                jax.ShapeDtypeStruct(queries.shape, BF16),
                jax.ShapeDtypeStruct(fast_weights.shape, F32),
                jax.ShapeDtypeStruct(fast_weights.shape, F32),
            ],
            in_specs=[VMEM] * few + [HBM] * (1 + len(before)),
            out_specs=[HBM] * 3,
            scratch_shapes=[
                pltpu.VMEM((few, out_rows, LANES), BF16),
                pltpu.VMEM((3, rows, slab), F32),
                pltpu.VMEM((tokens, slab), BF16),
                pltpu.VMEM((3, rows, slab), F32),
                pltpu.VMEM((3, rows, slab), F32),
                sem((3,)),
                sem((7,)),
            ],
            input_output_aliases={few + 1 + i: i for i in range(len(before))},
        )

    return tuple(outputs_of(FAR, pieces[:few], *outputs_of(NEAR, pieces[few:])))


def solution(mesh):
    in_specs = (
        P(("groups", "seq"), None),
        P(("groups", "seq"), None),
        P(("groups", "seq"), None),
        P(("groups", "seq"), None),
        P("seq", None),
        P(),
        P(),
    )
    out_specs = (P(("groups", "seq"), None), P(("groups", "seq"), None), P(("groups", "seq"), None))
    return jax.shard_map(shards, mesh=mesh, in_specs=in_specs, out_specs=out_specs, check_vma=False)
```

```python
import functools
import math

import jax
import jax.numpy as jnp
from jax import lax
from jax.experimental import pallas as pl
from jax.experimental.pallas import tpu as pltpu
from jax.sharding import PartitionSpec as P

WINDOW = 1024
LANES = 128
HALF = 64
VMEM_LIMIT = 24 * 1024 * 1024
FULL_VMEM = 58 * 1024 * 1024
BF16 = jnp.bfloat16
F32 = jnp.float32
I32 = jnp.int32
FAR = (4, 5, 6, 7)
NEAR = (2, 3, 1, 0)
BOTH = FAR + NEAR
KEY_ORDER = (4, 5, 2, 3, 1, 6, 7, 0)
HBM = pl.BlockSpec(memory_space=pltpu.HBM)
ANY = pl.BlockSpec(memory_space=pl.ANY)
VMEM = pl.BlockSpec(memory_space=pltpu.VMEM)


def tiles_of(head):
    first = (5 * head) // 2
    odd = head % 2
    return (first + odd) * LANES, (first if odd else first + 2) * LANES


def turned(tile):
    return pltpu.roll(tile, HALF, axis=1)


def low_lanes(rows):
    return lax.broadcasted_iota(I32, (rows, LANES), 1) < HALF


def dot(left, right, contract):
    return lax.dot_general(left, right, (contract, ((), ())), preferred_element_type=F32)


def chip_core(width):
    place = lax.axis_index("seq")
    return place // width, lax.rem(place, width)


def slot_of(index, slot):
    part = (index * (65536 // slot + (65536 % slot > 0))) >> 16
    return part, index - part * slot


def natural_row(row, odd):
    return jnp.where(odd == 1, jnp.where(row < 2 * LANES, row + HALF, row - 2 * LANES), row)


def copy_all(pairs, sems):
    copies = [pltpu.make_async_copy(src, dst, sems.at[i]) for i, (src, dst) in enumerate(pairs)]
    for copy in copies:
        copy.start()
    return copies


def pack_keys(width, heads, rows, slot, steps, k_hbm, v_hbm, step_hbm, fw_hbm, *rest):
    few = heads // 2
    outs, (k_ref, v_ref, step_ref, fw_ref, pay, wbuf, sems) = rest[:few], rest[few:]
    chip, _ = chip_core(width)
    side = (chip ^ steps[0]) // few
    slab = k_ref.shape[1]
    matrix = fw_hbm.shape[1] // 3
    at = pl.multiple_of(side * slab, LANES)
    pairs = [(k_hbm.at[:, pl.ds(at, slab)], k_ref), (v_hbm.at[:, pl.ds(at, slab)], v_ref), (step_hbm, step_ref)]
    for m in range(3):
        lane = pl.multiple_of(side * slab + m * matrix, LANES)
        pairs.append((fw_hbm.at[:, pl.ds(lane, slab)], fw_ref.at[m]))
    copies = copy_all(pairs, sems)
    tokens = k_ref.shape[0]
    low = low_lanes(tokens)
    low_r = low_lanes(rows)
    share = pl.multiple_of(lax.rem(lax.axis_index("groups"), 2) * (4 * slot), 8)
    for copy in copies:
        copy.wait()
    wbuf[...] = jnp.zeros_like(wbuf)
    for head in range(few):
        whole, half = tiles_of(head)
        odd = head % 2
        pay[head, 0:tokens] = k_ref[:, whole : whole + LANES]
        pay[head, tokens : 2 * tokens] = k_ref[:, whole + LANES : whole + 2 * LANES]
        pay[head, 3 * tokens : 4 * tokens] = v_ref[:, whole : whole + LANES]
        pay[head, 4 * tokens : 5 * tokens] = v_ref[:, whole + LANES : whole + 2 * LANES]
        k_half = k_ref[:, half : half + LANES].astype(F32)
        v_half = v_ref[:, half : half + LANES].astype(F32)
        mixed = jnp.where(low, turned(k_half) if odd else k_half, v_half if odd else turned(v_half))
        pay[head, 2 * tokens : 3 * tokens] = mixed.astype(BF16)
        halves = []
        for m in range(3):
            for t in range(2):
                spot = (2 * m + t) * slot
                wbuf[head, spot : spot + rows] = fw_ref[m, :, whole + t * LANES : whole + (t + 1) * LANES]
            halves.append(fw_ref[m, :, half : half + LANES])
        first, third, second = halves
        if odd:
            first, third = turned(first), turned(third)
        else:
            second = turned(second)
        wbuf[head, 6 * slot : 6 * slot + rows] = jnp.where(low_r, first, second)
        wbuf[head, 7 * slot : 7 * slot + rows] = jnp.where(low_r, third, 0.0)
        step = step_ref[pl.ds(side * few + head, 1)]
        high = step.astype(BF16).astype(F32)
        middle = (step - high).astype(BF16).astype(F32)
        wbuf[head, pl.ds(share + rows, 1)] = high
        wbuf[head, pl.ds(share + rows + 1, 1)] = middle
        wbuf[head, pl.ds(share + rows + 2, 1)] = step - high - middle
        pay[head, 5 * tokens :] = wbuf[head, pl.ds(share, 4 * slot)].astype(BF16)
    for i, k in enumerate(steps):
        outs[i][...] = pay[lax.rem(chip ^ k, few)]


def pack_queries(width, heads, q_ref, *rest):
    outs, (pay,) = rest[:heads], rest[heads:]
    chip, _ = chip_core(width)
    tokens = q_ref.shape[0]
    mid = tokens // 2
    low = low_lanes(mid)
    for head in range(heads):
        whole, half = tiles_of(head)
        pay[head, 0:tokens] = q_ref[:, whole : whole + LANES]
        pay[head, tokens : 2 * tokens] = q_ref[:, whole + LANES : whole + 2 * LANES]
        top = q_ref[0:mid, half : half + LANES].astype(F32)
        bottom = q_ref[mid:, half : half + LANES].astype(F32)
        if head % 2:
            top = turned(top)
        else:
            bottom = turned(bottom)
        pay[head, 2 * tokens :] = jnp.where(low, top, bottom).astype(BF16)
    for i, k in enumerate(FAR + NEAR):
        outs[i][...] = pay[chip ^ k]


def pack_weights(heads, tokens, *refs):
    ins, out_ref = refs[:heads], refs[heads]
    size = ins[0].shape[0] - 5 * tokens
    for i, k in enumerate(KEY_ORDER):
        out_ref[k * size : (k + 1) * size] = ins[i][5 * tokens :]


def key_side(width, heads, rows, slot, tokens, scale, *refs):
    count = heads * width
    ins = refs[:count]
    shared = refs[count : count + width]
    grad_ref, copy_ref, kv_ref = refs[count + width : count + width + 3]
    gates, hidden, target = refs[count + width + 3 :]
    chip, core = chip_core(width)
    odd = lax.rem(chip, 2)
    wide = 3 * LANES
    size = rows * count
    place = {k: i for i, k in enumerate(KEY_ORDER)}
    blocks = [ins[other * heads + place[k]] for other in range(width) for k in range(heads)]
    for index, block in enumerate(blocks):
        other, k = divmod(index, heads)
        kv_ref[(chip ^ k) * width + (core ^ other)] = block[0 : 5 * tokens]
    parts = [block[5 * tokens :].astype(F32) for block in blocks]
    column, row_in = slot_of(lax.broadcasted_iota(I32, (wide, count * slot), 1), slot)
    source = ((column & (heads - 1)) ^ chip) * width + (core ^ (column >> (heads.bit_length() - 1)))
    wanted = lax.broadcasted_iota(I32, (wide, count * slot), 0)
    chosen = (source * rows + row_in == natural_row(wanted, odd)) & (row_in < rows) & (wanted < size)
    chosen = jnp.where(chosen, 1.0, 0.0).astype(BF16)
    size_4 = 4 * slot
    others = [shared[i // heads][(i % heads) * size_4 : (i % heads + 1) * size_4].astype(F32) for i in range(count)]
    gathered = [
        jnp.concatenate([part[t * slot : (t + 1) * slot] for part in source], axis=0).astype(BF16)
        for source in (parts, others)
        for t in range(4)
    ]
    placed = dot(chosen, jnp.concatenate(gathered, axis=1), ((1,), (0,)))
    mine, theirs = placed[:, : 4 * LANES], placed[:, 4 * LANES :]
    first_share = lax.rem(lax.axis_index("groups"), 2) == 0
    tile = [jnp.where(first_share, mine, theirs), jnp.where(first_share, theirs, mine)]
    tile = [part[:, t * LANES : (t + 1) * LANES] for part in tile for t in range(4)]
    low = low_lanes(wide)
    columns = [tile[0], tile[1], jnp.where(low, tile[6], 0.0), tile[2], tile[3], tile[7]]
    columns += [jnp.where(low, 0.0, tile[6]), tile[4], tile[5]]
    for t, column_tile in enumerate(columns):
        copy_ref[:, t * LANES : (t + 1) * LANES] = column_tile.astype(BF16)

    steps = [jnp.sum(part[rows : rows + 3], axis=0, keepdims=True) for part in parts[:heads]]
    steps = jnp.concatenate(steps, axis=0).T
    w13 = copy_ref[:, 0 : 2 * wide]
    w2 = copy_ref[:, 2 * wide :]
    for j in range(heads):
        block = blocks[j]
        keys = jnp.concatenate([block[t * tokens : (t + 1) * tokens] for t in range(3)], axis=1)
        values = jnp.concatenate([block[t * tokens : (t + 1) * tokens] for t in range(2, 5)], axis=1)
        at = j * tokens
        tgt = (-steps[:, j : j + 1] * values.astype(F32)).astype(BF16)
        both = dot(keys, w13, ((1,), (0,))) * scale
        back = dot(tgt, w2, ((1,), (1,))) * scale
        gate, up = both[:, :wide], both[:, wide:]
        sig = 1.0 / (1.0 + jnp.exp(-gate))
        silu = gate * sig
        gates[at : at + tokens, 0:wide] = (back * up * (sig * (1.0 + gate * (1.0 - sig)))).astype(BF16)
        gates[at : at + tokens, wide:] = (back * silu).astype(BF16)
        hidden[at : at + tokens] = (silu * up).astype(BF16)
        target[at : at + tokens] = tgt
    all_keys = [
        jnp.concatenate([blocks[j][t * tokens : (t + 1) * tokens] for t in range(3)], axis=1) for j in range(heads)
    ]
    grads13 = dot(jnp.concatenate(all_keys, axis=0), gates[...], ((0,), (0,))) * scale
    grads2 = dot(hidden[...], target[...], ((0,), (0,))) * scale
    grad_ref[:, 0 : 2 * wide] = grads13[0:size]
    grad_ref[:, 2 * wide :] = grads2[0:size]


def query_side(width, heads, tokens, scale, span, steps, *refs):
    few = heads // 2
    kv_ref, copy_ref, fast_gain_ref, window_gain_ref = refs[:4]
    qs = refs[4 : 4 + few]
    outs, (qbuf, pay) = refs[-(few + 2) : -2], refs[-2:]
    chip, core = chip_core(width)
    for i, k in enumerate(steps):
        qbuf[lax.rem(chip ^ k, few)] = qs[i][...]
    wide = 3 * LANES
    mid = tokens // 2
    low = low_lanes(mid)
    high = jnp.logical_not(low_lanes(2 * tokens))
    size = heads * 40

    def query_block(j):
        tail = qbuf[j, 2 * tokens :].astype(F32)
        half = jnp.concatenate([jnp.where(low, tail, 0.0), jnp.where(low, turned(tail), 0.0)], axis=0)
        return jnp.concatenate([qbuf[j, 0:tokens], qbuf[j, tokens : 2 * tokens], half.astype(BF16)], axis=1)

    def two_blocks(j):
        place = j * width + core
        slot = j % few
        q = jnp.concatenate([query_block(slot), query_block(slot + 1)], axis=0)
        blocks = min(width * (j + 2), span + 1 + width)
        start = 0 if blocks == width * (j + 2) else jnp.maximum(place - span, 0)
        keys_seen = blocks * tokens
        seen = kv_ref[pl.ds(start, blocks)]
        tiles = [seen[:, t * tokens : (t + 1) * tokens].reshape(keys_seen, LANES) for t in range(5)]
        row = lax.broadcasted_iota(I32, (2 * tokens, 1), 0)
        row = jnp.where(row < tokens, row, row + (width - 1) * tokens) + (place - start) * tokens
        distance = row - lax.broadcasted_iota(I32, (2 * tokens, keys_seen), 1)
        allowed = distance >= 0
        if keys_seen > span * tokens:
            allowed = allowed & (distance < span * tokens)
        score = dot(q, jnp.concatenate(tiles[0:3], axis=1), ((1,), (1,)))
        score = jnp.where(allowed, score, -jnp.inf)
        top = jnp.max(score, axis=1, keepdims=True)
        weight = jnp.exp2((score - top) * (scale * math.log2(math.e)))
        total = jnp.sum(weight, axis=1, keepdims=True)
        attended = dot(weight.astype(BF16), jnp.concatenate(tiles[2:5], axis=1), ((1,), (0,))) / total
        attended = jnp.concatenate([jnp.where(high, attended[:, 0:LANES], 0.0), attended[:, LANES:]], axis=1)
        mean_sq = jnp.sum(attended * attended, axis=1, keepdims=True) * (1.0 / size)
        window_part = attended * lax.rsqrt(mean_sq + 1e-05) * window_gain_ref[...]

        both = dot(q, copy_ref[:, 0 : 2 * wide], ((1,), (0,))) * scale
        gate, up = both[:, :wide], both[:, wide:]
        hid = (gate / (1.0 + jnp.exp(-gate)) * up).astype(BF16)
        out = dot(hid, copy_ref[:, 2 * wide :], ((1,), (0,))) * scale
        mean_sq = jnp.sum(out * out, axis=1, keepdims=True) * (1.0 / size)
        layer = out * lax.rsqrt(mean_sq + 1e-05) * fast_gain_ref[...] + window_part
        for i in range(2):
            part = layer[i * tokens : (i + 1) * tokens]
            pay[slot + i, 0:tokens] = part[:, LANES : 2 * LANES].astype(BF16)
            pay[slot + i, tokens : 2 * tokens] = part[:, 2 * LANES :].astype(BF16)
            pay[slot + i, 2 * tokens :] = jnp.where(
                low, turned(part[mid:, 0:LANES]), part[0:mid, 0:LANES]
            ).astype(BF16)

    first_half = (chip ^ steps[0]) < few

    @pl.when(first_half)
    def _():
        for j in range(0, few, 2):
            two_blocks(j)

    @pl.when(jnp.logical_not(first_half))
    def _():
        for j in range(few, heads, 2):
            two_blocks(j)

    for i, k in enumerate(steps):
        outs[i][...] = pay[lax.rem(chip ^ k, few)]


def pack_momentum(width, heads, rows, slot, *refs):
    grads = refs[:width]
    copy_ref = refs[width]
    layers = refs[width + 1 : width + 1 + heads]
    outs = refs[width + 1 + heads : width + 1 + 2 * heads]
    (pay,) = refs[width + 1 + 2 * heads :]
    chip, core = chip_core(width)
    odd = lax.rem(chip, 2)
    size = rows * heads * width
    wide = 3 * LANES
    summed = grads[0][...]
    for other in grads[1:]:
        summed = summed + other[...]
    rounded = summed.astype(BF16)
    old = copy_ref[0:size].astype(F32)
    moved = old - rounded.astype(F32)
    ratio = (jnp.sum(old * old, axis=0, keepdims=True) + 1e-06) / (jnp.sum(moved * moved, axis=0, keepdims=True) + 1e-06)
    ratio = jnp.sqrt(ratio)
    ratio_high = ratio.astype(BF16).astype(F32)
    head, row_in = slot_of(lax.broadcasted_iota(I32, (heads * slot, size), 0), slot)
    wanted = (head * width + core) * rows + row_in
    chosen = (wanted == natural_row(lax.broadcasted_iota(I32, (heads * slot, size), 1), odd)) & (row_in < rows)
    picked = dot(jnp.where(chosen, 1.0, 0.0).astype(BF16), rounded, ((1,), (0,)))
    _, row_in = slot_of(lax.broadcasted_iota(I32, (heads * slot, 1), 0), slot)
    picked = jnp.where(row_in == rows, ratio_high, jnp.where(row_in == rows + 1, ratio - ratio_high, picked))
    tile = [picked[:, t * LANES : (t + 1) * LANES] for t in range(9)]
    low = low_lanes(heads * slot)
    order = [tile[0], tile[1], tile[3], tile[4], tile[7], tile[8], jnp.where(low, tile[2], tile[6]), tile[5]]
    for b in range(heads):
        pay[b] = jnp.concatenate([part[b * slot : (b + 1) * slot] for part in order], axis=0).astype(BF16)
    for i, k in enumerate(FAR + NEAR):
        cut = layers[i].shape[0]
        outs[i][0:cut] = layers[i][...]
        outs[i][cut:] = pay[chip ^ k]


def unpack(width, heads, rows, slot, tokens, *refs):
    pieces = refs[:heads]
    fw_ref, layer_hbm, new_hbm, momentum_hbm, buf, layer_ref, new_ref, momentum_ref, sems = refs[heads:]
    chip, _ = chip_core(width)
    matrix = fw_ref.shape[1] // 3
    for i, k in enumerate(KEY_ORDER):
        buf[chip ^ k] = pieces[i][...]
    mid = tokens // 2
    cut = 2 * tokens + mid
    low = low_lanes(mid)
    low_r = low_lanes(slot)

    def write(lane, block):
        moment = block[0:rows]
        factor = block[rows : rows + 1] + block[rows + 1 : rows + 2]
        momentum_ref[:, lane : lane + LANES] = moment
        new_ref[:, lane : lane + LANES] = (fw_ref[:, lane : lane + LANES] - moment) * factor

    moments = [buf[head, cut:].astype(F32) for head in range(heads)]
    for head in range(heads):
        whole, half = tiles_of(head)
        for m in range(3):
            for t in range(2):
                write(m * matrix + whole + t * LANES, moments[head][(2 * m + t) * slot : (2 * m + t + 1) * slot])
    for head in range(0, heads, 2):
        _, half = tiles_of(head)
        even = moments[head][6 * slot : 7 * slot]
        odd = moments[head + 1][6 * slot : 7 * slot]
        write(half, jnp.where(low_r, even, turned(odd)))
        write(2 * matrix + half, jnp.where(low_r, turned(even), odd))
        even = moments[head][7 * slot :]
        odd = moments[head + 1][7 * slot :]
        write(matrix + half, jnp.where(low_r, even, turned(odd)))
    writes = copy_all([(new_ref, new_hbm), (momentum_ref, momentum_hbm)], sems)
    for head in range(heads):
        whole, half = tiles_of(head)
        layer_ref[:, whole : whole + LANES] = buf[head, 0:tokens]
        layer_ref[:, whole + LANES : whole + 2 * LANES] = buf[head, tokens : 2 * tokens]
    for head in range(0, heads, 2):
        _, half = tiles_of(head)
        even = buf[head, 2 * tokens : cut].astype(F32)
        odd = buf[head + 1, 2 * tokens : cut].astype(F32)
        layer_ref[0:mid, half : half + LANES] = jnp.where(low, turned(even), odd).astype(BF16)
        layer_ref[mid:, half : half + LANES] = jnp.where(low, even, turned(odd)).astype(BF16)
    for copy in writes + copy_all([(layer_ref, layer_hbm)], sems.at[pl.ds(2, 1)]):
        copy.wait()


def shards(queries, key_vectors, value_vectors, step_sizes, fast_weights, fast_gain, window_gain):
    tokens = queries.shape[0]
    heads = step_sizes.shape[1]
    few = heads // 2
    head_width = queries.shape[1] // heads
    scale = 1.0 / math.sqrt(head_width)
    count = lax.axis_size("seq")
    width = count // heads
    rows = fast_weights.shape[0]
    slot = -(-(rows + 3) // 8) * 8
    span = WINDOW // tokens
    wide = 3 * LANES
    slab = few * head_width
    sem = pltpu.SemaphoreType.DMA
    key_rows = 5 * tokens + 4 * slot
    query_rows = 2 * tokens + tokens // 2
    out_rows = query_rows + 8 * slot

    def across(value, step):
        return lax.ppermute(value, "seq", [(i, i ^ step) for i in range(count)])

    def exchange(pieces, steps):
        return [across(piece, k * width) if k else piece for piece, k in zip(pieces, steps)]

    def packed(size, many):
        return [jax.ShapeDtypeStruct((size, LANES), BF16)] * many

    def cost(micros):
        return pl.CostEstimate(flops=micros * 500_000_000, transcendentals=0, bytes_accessed=micros * 2_000_000)

    def call(body, name, micros, *operands, grant=VMEM_LIMIT, **kwargs):
        params = pltpu.CompilerParams(vmem_limit_bytes=grant)
        return pl.pallas_call(
            body, compiler_params=params, cost_estimate=cost(micros), name=name, **kwargs
        )(*operands)

    step_rows = step_sizes.T

    def keys_for(steps):
        return call(
            functools.partial(pack_keys, width, heads, rows, slot, steps),
            "pack_keys",
            2,
            key_vectors,
            value_vectors,
            step_rows,
            fast_weights,
            grant=FULL_VMEM if steps == FAR else VMEM_LIMIT,
            out_shape=packed(key_rows, few),
            in_specs=[HBM] * 4,
            out_specs=[VMEM] * few,
            scratch_shapes=[
                pltpu.VMEM((tokens, slab), BF16),
                pltpu.VMEM((tokens, slab), BF16),
                pltpu.VMEM((heads, tokens), F32),
                pltpu.VMEM((3, rows, slab), F32),
                pltpu.VMEM((few, key_rows, LANES), BF16),
                pltpu.VMEM((few, 8 * slot, LANES), F32),
                sem((6,)),
            ],
        )

    key_pieces = dict(zip(BOTH, keys_for(FAR) + keys_for(NEAR)))
    key_blocks = exchange([key_pieces[k] for k in KEY_ORDER], KEY_ORDER)
    for other in range(1, width):
        key_blocks = key_blocks + [across(block, other) for block in key_blocks[:heads]]
    shared = call(
        functools.partial(pack_weights, heads, tokens),
        "pack_weights",
        0,
        *key_blocks[:heads],
        out_shape=jax.ShapeDtypeStruct((heads * 4 * slot, LANES), BF16),
        in_specs=[VMEM] * heads,
        out_specs=VMEM,
    )
    shared = lax.ppermute(shared, "groups", [(i, i ^ 1) for i in range(lax.axis_size("groups"))])
    shared = [shared] + [across(shared, other) for other in range(1, width)]
    query_pieces = call(
        functools.partial(pack_queries, width, heads),
        "pack_queries",
        1,
        queries,
        out_shape=packed(query_rows, heads),
        in_specs=[VMEM],
        out_specs=[VMEM] * heads,
        scratch_shapes=[pltpu.VMEM((heads, query_rows, LANES), BF16)],
    )
    query_blocks = exchange(query_pieces, FAR + NEAR)

    gradient, copies, key_values = call(
        functools.partial(key_side, width, heads, rows, slot, tokens, scale),
        "key_side",
        0,
        *key_blocks,
        *shared,
        out_shape=[
            jax.ShapeDtypeStruct((head_width, 3 * wide), F32),
            jax.ShapeDtypeStruct((wide, 3 * wide), BF16),
            jax.ShapeDtypeStruct((count, 5 * tokens, LANES), BF16),
        ],
        in_specs=[VMEM] * (count + width),
        out_specs=[VMEM] * 3,
        scratch_shapes=[
            pltpu.VMEM((heads * tokens, 2 * wide), BF16),
            pltpu.VMEM((heads * tokens, wide), BF16),
            pltpu.VMEM((heads * tokens, wide), BF16),
        ],
    )
    gradients = [across(gradient, other) for other in range(1, width)]

    head = lax.axis_index("seq") // width
    odd = head % 2

    def gain_row(gain):
        row = lax.dynamic_slice_in_dim(gain.reshape(heads, head_width), head, 1, 0)
        gap = jnp.zeros((1, HALF), F32)
        even_row = jnp.concatenate([gap, row[:, 2 * LANES :], row[:, : 2 * LANES]], axis=1)
        odd_row = jnp.concatenate([gap, row], axis=1)
        return jnp.where(odd == 1, odd_row, even_row)

    gains = (gain_row(fast_gain), gain_row(window_gain))

    def layers_of(steps, blocks, micros):
        return call(
            functools.partial(query_side, width, heads, tokens, scale, span, steps),
            "query_side",
            micros,
            key_values,
            copies,
            *gains,
            *blocks,
            out_shape=packed(query_rows, few),
            in_specs=[VMEM] * (4 + few),
            out_specs=[VMEM] * few,
            scratch_shapes=[
                pltpu.VMEM((few, query_rows, LANES), BF16),
                pltpu.VMEM((few, query_rows, LANES), BF16),
            ],
        )

    near_layers = layers_of(NEAR, query_blocks[few:], 0)
    far_layers = layers_of(FAR, query_blocks[:few], 40)
    pieces = call(
        functools.partial(pack_momentum, width, heads, rows, slot),
        "pack_momentum",
        2,
        gradient,
        *gradients,
        copies,
        *far_layers,
        *near_layers,
        out_shape=packed(out_rows, heads),
        in_specs=[VMEM] * (width + 1 + heads),
        out_specs=[VMEM] * heads,
        scratch_shapes=[pltpu.VMEM((heads, 8 * slot, LANES), BF16)],
    )
    pieces = dict(zip(BOTH, pieces))
    pieces = exchange([pieces[k] for k in KEY_ORDER], KEY_ORDER)

    return tuple(
        call(
            functools.partial(unpack, width, heads, rows, slot, tokens),
            "unpack",
            2,
            *pieces,
            fast_weights,
            out_shape=[
                jax.ShapeDtypeStruct(queries.shape, BF16),
                jax.ShapeDtypeStruct(fast_weights.shape, F32),
                jax.ShapeDtypeStruct(fast_weights.shape, F32),
            ],
            in_specs=[VMEM] * (heads + 1),
            out_specs=[HBM] * 3,
            scratch_shapes=[
                pltpu.VMEM((heads, out_rows, LANES), BF16),
                pltpu.VMEM(queries.shape, BF16),
                pltpu.VMEM(fast_weights.shape, F32),
                pltpu.VMEM(fast_weights.shape, F32),
                sem((3,)),
            ],
        )
    )


def solution(mesh):
    in_specs = (
        P(("groups", "seq"), None),
        P(("groups", "seq"), None),
        P(("groups", "seq"), None),
        P(("groups", "seq"), None),
        P("seq", None),
        P(),
        P(),
    )
    out_specs = (P(("groups", "seq"), None), P(("groups", "seq"), None), P(("groups", "seq"), None))
    return jax.shard_map(shards, mesh=mesh, in_specs=in_specs, out_specs=out_specs, check_vma=False)
```

```python
import functools
import math

import jax
import jax.numpy as jnp
from jax import lax
from jax.experimental import pallas as pl
from jax.experimental.pallas import tpu as pltpu
from jax.sharding import PartitionSpec as P

WINDOW = 1024
LANES = 128
HALF = 64
VMEM_LIMIT = 24 * 1024 * 1024
FULL_VMEM = 58 * 1024 * 1024
BF16 = jnp.bfloat16
F32 = jnp.float32
I32 = jnp.int32
FAR = (4, 5, 6, 7)
NEAR = (2, 3, 1, 0)
BOTH = FAR + NEAR
KEY_ORDER = (7, 5, 2, 3, 1, 4, 6, 0)
OUT_ORDER = (4, 5, 2, 3, 1, 6, 7, 0)
HBM = pl.BlockSpec(memory_space=pltpu.HBM)
ANY = pl.BlockSpec(memory_space=pl.ANY)
VMEM = pl.BlockSpec(memory_space=pltpu.VMEM)


def tiles_of(head):
    first = (5 * head) // 2
    odd = head % 2
    return (first + odd) * LANES, (first if odd else first + 2) * LANES


def turned(tile):
    return pltpu.roll(tile, HALF, axis=1)


def low_lanes(rows):
    return lax.broadcasted_iota(I32, (rows, LANES), 1) < HALF


def dot(left, right, contract):
    return lax.dot_general(left, right, (contract, ((), ())), preferred_element_type=F32)


def chip_core(width):
    place = lax.axis_index("seq")
    return place // width, lax.rem(place, width)


def slot_of(index, slot):
    part = (index * (65536 // slot + (65536 % slot > 0))) >> 16
    return part, index - part * slot


def natural_row(row, odd):
    return jnp.where(odd == 1, jnp.where(row < 2 * LANES, row + HALF, row - 2 * LANES), row)


def copy_all(pairs, sems):
    copies = [pltpu.make_async_copy(src, dst, sems.at[i]) for i, (src, dst) in enumerate(pairs)]
    for copy in copies:
        copy.start()
    return copies


def pack_keys(width, heads, rows, slot, steps, k_hbm, v_hbm, step_hbm, fw_hbm, *rest):
    few = heads // 2
    outs, (k_ref, v_ref, step_ref, fw_ref, pay, wbuf, sems) = rest[:few], rest[few:]
    chip, _ = chip_core(width)
    side = (chip ^ steps[0]) // few
    slab = k_ref.shape[1]
    matrix = fw_hbm.shape[1] // 3
    at = pl.multiple_of(side * slab, LANES)
    pairs = [(k_hbm.at[:, pl.ds(at, slab)], k_ref), (v_hbm.at[:, pl.ds(at, slab)], v_ref), (step_hbm, step_ref)]
    for m in range(3):
        lane = pl.multiple_of(side * slab + m * matrix, LANES)
        pairs.append((fw_hbm.at[:, pl.ds(lane, slab)], fw_ref.at[m]))
    copies = copy_all(pairs, sems)
    tokens = k_ref.shape[0]
    low = low_lanes(tokens)
    low_r = low_lanes(rows)
    share = pl.multiple_of(lax.rem(lax.axis_index("groups"), 2) * (4 * slot), 8)
    for copy in copies:
        copy.wait()
    wbuf[...] = jnp.zeros_like(wbuf)
    for head in range(few):
        whole, half = tiles_of(head)
        odd = head % 2
        pay[head, 0:tokens] = k_ref[:, whole : whole + LANES]
        pay[head, tokens : 2 * tokens] = k_ref[:, whole + LANES : whole + 2 * LANES]
        pay[head, 3 * tokens : 4 * tokens] = v_ref[:, whole : whole + LANES]
        pay[head, 4 * tokens : 5 * tokens] = v_ref[:, whole + LANES : whole + 2 * LANES]
        k_half = k_ref[:, half : half + LANES].astype(F32)
        v_half = v_ref[:, half : half + LANES].astype(F32)
        mixed = jnp.where(low, turned(k_half) if odd else k_half, v_half if odd else turned(v_half))
        pay[head, 2 * tokens : 3 * tokens] = mixed.astype(BF16)
        halves = []
        for m in range(3):
            for t in range(2):
                spot = (2 * m + t) * slot
                wbuf[head, spot : spot + rows] = fw_ref[m, :, whole + t * LANES : whole + (t + 1) * LANES]
            halves.append(fw_ref[m, :, half : half + LANES])
        first, third, second = halves
        if odd:
            first, third = turned(first), turned(third)
        else:
            second = turned(second)
        wbuf[head, 6 * slot : 6 * slot + rows] = jnp.where(low_r, first, second)
        wbuf[head, 7 * slot : 7 * slot + rows] = jnp.where(low_r, third, 0.0)
        step = step_ref[pl.ds(side * few + head, 1)]
        high = step.astype(BF16).astype(F32)
        middle = (step - high).astype(BF16).astype(F32)
        wbuf[head, pl.ds(share + rows, 1)] = high
        wbuf[head, pl.ds(share + rows + 1, 1)] = middle
        wbuf[head, pl.ds(share + rows + 2, 1)] = step - high - middle
        pay[head, 5 * tokens :] = wbuf[head, pl.ds(share, 4 * slot)].astype(BF16)
    for i, k in enumerate(steps):
        outs[i][...] = pay[lax.rem(chip ^ k, few)]


def pack_queries(width, heads, q_ref, *rest):
    outs, (pay,) = rest[:heads], rest[heads:]
    chip, _ = chip_core(width)
    tokens = q_ref.shape[0]
    mid = tokens // 2
    low = low_lanes(mid)
    for head in range(heads):
        whole, half = tiles_of(head)
        pay[head, 0:tokens] = q_ref[:, whole : whole + LANES]
        pay[head, tokens : 2 * tokens] = q_ref[:, whole + LANES : whole + 2 * LANES]
        top = q_ref[0:mid, half : half + LANES].astype(F32)
        bottom = q_ref[mid:, half : half + LANES].astype(F32)
        if head % 2:
            top = turned(top)
        else:
            bottom = turned(bottom)
        pay[head, 2 * tokens :] = jnp.where(low, top, bottom).astype(BF16)
    for i, k in enumerate(FAR + NEAR):
        outs[i][...] = pay[chip ^ k]


def pack_weights(heads, tokens, *refs):
    ins, out_ref = refs[:heads], refs[heads]
    size = ins[0].shape[0] - 5 * tokens
    for i, k in enumerate(KEY_ORDER):
        out_ref[k * size : (k + 1) * size] = ins[i][5 * tokens :]


def key_side(width, heads, rows, slot, tokens, scale, *refs):
    count = heads * width
    ins = refs[:count]
    shared = refs[count : count + width]
    grad_ref, copy_ref, kv_ref = refs[count + width : count + width + 3]
    gates, hidden, target = refs[count + width + 3 :]
    chip, core = chip_core(width)
    odd = lax.rem(chip, 2)
    wide = 3 * LANES
    size = rows * count
    place = {k: i for i, k in enumerate(KEY_ORDER)}
    blocks = [ins[other * heads + place[k]] for other in range(width) for k in range(heads)]
    for index, block in enumerate(blocks):
        other, k = divmod(index, heads)
        kv_ref[(chip ^ k) * width + (core ^ other)] = block[0 : 5 * tokens]
    parts = [block[5 * tokens :].astype(F32) for block in blocks]
    column, row_in = slot_of(lax.broadcasted_iota(I32, (wide, count * slot), 1), slot)
    source = ((column & (heads - 1)) ^ chip) * width + (core ^ (column >> (heads.bit_length() - 1)))
    wanted = lax.broadcasted_iota(I32, (wide, count * slot), 0)
    chosen = (source * rows + row_in == natural_row(wanted, odd)) & (row_in < rows) & (wanted < size)
    chosen = jnp.where(chosen, 1.0, 0.0).astype(BF16)
    size_4 = 4 * slot
    others = [shared[i // heads][(i % heads) * size_4 : (i % heads + 1) * size_4].astype(F32) for i in range(count)]
    gathered = [
        jnp.concatenate([part[t * slot : (t + 1) * slot] for part in source], axis=0).astype(BF16)
        for source in (parts, others)
        for t in range(4)
    ]
    placed = dot(chosen, jnp.concatenate(gathered, axis=1), ((1,), (0,)))
    mine, theirs = placed[:, : 4 * LANES], placed[:, 4 * LANES :]
    first_share = lax.rem(lax.axis_index("groups"), 2) == 0
    tile = [jnp.where(first_share, mine, theirs), jnp.where(first_share, theirs, mine)]
    tile = [part[:, t * LANES : (t + 1) * LANES] for part in tile for t in range(4)]
    low = low_lanes(wide)
    columns = [tile[0], tile[1], jnp.where(low, tile[6], 0.0), tile[2], tile[3], tile[7]]
    columns += [jnp.where(low, 0.0, tile[6]), tile[4], tile[5]]
    for t, column_tile in enumerate(columns):
        copy_ref[:, t * LANES : (t + 1) * LANES] = column_tile.astype(BF16)

    steps = [jnp.sum(part[rows : rows + 3], axis=0, keepdims=True) for part in parts[:heads]]
    steps = jnp.concatenate(steps, axis=0).T
    w13 = copy_ref[:, 0 : 2 * wide]
    w2 = copy_ref[:, 2 * wide :]
    for j in range(heads):
        block = blocks[j]
        keys = jnp.concatenate([block[t * tokens : (t + 1) * tokens] for t in range(3)], axis=1)
        values = jnp.concatenate([block[t * tokens : (t + 1) * tokens] for t in range(2, 5)], axis=1)
        at = j * tokens
        tgt = (-steps[:, j : j + 1] * values.astype(F32)).astype(BF16)
        both = dot(keys, w13, ((1,), (0,))) * scale
        back = dot(tgt, w2, ((1,), (1,))) * scale
        gate, up = both[:, :wide], both[:, wide:]
        sig = 0.5 + 0.5 * jnp.tanh(0.5 * gate)
        silu = gate * sig
        gates[at : at + tokens, 0:wide] = (back * up * (sig * (1.0 + gate * (1.0 - sig)))).astype(BF16)
        gates[at : at + tokens, wide:] = (back * silu).astype(BF16)
        hidden[at : at + tokens] = (silu * up).astype(BF16)
        target[at : at + tokens] = tgt
    all_keys = [
        jnp.concatenate([blocks[j][t * tokens : (t + 1) * tokens] for t in range(3)], axis=1) for j in range(heads)
    ]
    grads13 = dot(jnp.concatenate(all_keys, axis=0), gates[...], ((0,), (0,))) * scale
    grads2 = dot(hidden[...], target[...], ((0,), (0,))) * scale
    grad_ref[:, 0 : 2 * wide] = grads13[0:size]
    grad_ref[:, 2 * wide :] = grads2[0:size]


def query_side(width, heads, tokens, scale, span, steps, *refs):
    few = heads // 2
    kv_ref, copy_ref, fast_gain_ref, window_gain_ref = refs[:4]
    qs = refs[4 : 4 + few]
    outs, (qbuf, pay) = refs[-(few + 2) : -2], refs[-2:]
    chip, core = chip_core(width)
    for i, k in enumerate(steps):
        qbuf[lax.rem(chip ^ k, few)] = qs[i][...]
    wide = 3 * LANES
    mid = tokens // 2
    low = low_lanes(mid)
    high = jnp.logical_not(low_lanes(2 * tokens))
    size = heads * 40

    def query_block(j):
        tail = qbuf[j, 2 * tokens :].astype(F32)
        half = jnp.concatenate([jnp.where(low, tail, 0.0), jnp.where(low, turned(tail), 0.0)], axis=0)
        return jnp.concatenate([qbuf[j, 0:tokens], qbuf[j, tokens : 2 * tokens], half.astype(BF16)], axis=1)

    def two_blocks(j):
        place = j * width + core
        slot = j % few
        q = jnp.concatenate([query_block(slot), query_block(slot + 1)], axis=0)
        blocks = min(width * (j + 2), span + 1 + width)
        start = 0 if blocks == width * (j + 2) else jnp.maximum(place - span, 0)
        keys_seen = blocks * tokens
        seen = kv_ref[pl.ds(start, blocks)]
        tiles = [seen[:, t * tokens : (t + 1) * tokens].reshape(keys_seen, LANES) for t in range(5)]
        row = lax.broadcasted_iota(I32, (2 * tokens, 1), 0)
        row = jnp.where(row < tokens, row, row + (width - 1) * tokens) + (place - start) * tokens
        score = dot(q, jnp.concatenate(tiles[0:3], axis=1), ((1,), (1,)))

        def masked(first, last):
            distance = row - lax.broadcasted_iota(I32, (2 * tokens, (last - first) * tokens), 1) - first * tokens
            allowed = distance >= 0
            if keys_seen > span * tokens:
                allowed = allowed & (distance < span * tokens)
            return jnp.where(allowed, score[:, first * tokens : last * tokens], -jnp.inf)

        whole = (width + 1, span) if keys_seen > span * tokens else (0, width * j)
        if whole[0] < whole[1]:
            parts = [masked(0, whole[0])] if whole[0] else []
            parts += [score[:, whole[0] * tokens : whole[1] * tokens], masked(whole[1], blocks)]
            score = jnp.concatenate(parts, axis=1)
        else:
            score = masked(0, blocks)
        top = jnp.max(score, axis=1, keepdims=True)
        weight = jnp.exp2((score - top) * (scale * math.log2(math.e)))
        total = jnp.sum(weight, axis=1, keepdims=True)
        attended = dot(weight.astype(BF16), jnp.concatenate(tiles[2:5], axis=1), ((1,), (0,)))
        attended = jnp.concatenate([jnp.where(high, attended[:, 0:LANES], 0.0), attended[:, LANES:]], axis=1)
        share = 1.0 / total
        mean_sq = jnp.sum(attended * attended, axis=1, keepdims=True) * (share * share * (1.0 / size))
        window_part = attended * (share * lax.rsqrt(mean_sq + 1e-05)) * window_gain_ref[...]

        both = dot(q, copy_ref[:, 0 : 2 * wide], ((1,), (0,)))
        gate, up = both[:, :wide], both[:, wide:]
        hid = (gate * up * (0.5 * scale * scale) * (1.0 + jnp.tanh(gate * (0.5 * scale)))).astype(BF16)
        out = dot(hid, copy_ref[:, 2 * wide :], ((1,), (0,)))
        mean_sq = jnp.sum(out * out, axis=1, keepdims=True) * (scale * scale / size)
        layer = out * (scale * lax.rsqrt(mean_sq + 1e-05)) * fast_gain_ref[...] + window_part
        for i in range(2):
            part = layer[i * tokens : (i + 1) * tokens]
            pay[slot + i, 0:tokens] = part[:, LANES : 2 * LANES].astype(BF16)
            pay[slot + i, tokens : 2 * tokens] = part[:, 2 * LANES :].astype(BF16)
            pay[slot + i, 2 * tokens :] = jnp.where(
                low, turned(part[mid:, 0:LANES]), part[0:mid, 0:LANES]
            ).astype(BF16)

    first_half = (chip ^ steps[0]) < few

    @pl.when(first_half)
    def _():
        for j in range(0, few, 2):
            two_blocks(j)

    @pl.when(jnp.logical_not(first_half))
    def _():
        for j in range(few, heads, 2):
            two_blocks(j)

    for i, k in enumerate(steps):
        outs[i][...] = pay[lax.rem(chip ^ k, few)]


def pack_momentum(width, heads, rows, slot, *refs):
    grads = refs[:width]
    copy_ref = refs[width]
    layers = refs[width + 1 : width + 1 + heads]
    outs = refs[width + 1 + heads : width + 1 + 2 * heads]
    (pay,) = refs[width + 1 + 2 * heads :]
    chip, core = chip_core(width)
    odd = lax.rem(chip, 2)
    size = rows * heads * width
    wide = 3 * LANES
    summed = grads[0][...]
    for other in grads[1:]:
        summed = summed + other[...]
    rounded = summed.astype(BF16)
    old = copy_ref[0:size].astype(F32)
    moved = old - rounded.astype(F32)
    ratio = (jnp.sum(old * old, axis=0, keepdims=True) + 1e-06) / (jnp.sum(moved * moved, axis=0, keepdims=True) + 1e-06)
    ratio = jnp.sqrt(ratio)
    ratio_high = ratio.astype(BF16).astype(F32)
    head, row_in = slot_of(lax.broadcasted_iota(I32, (heads * slot, size), 0), slot)
    wanted = (head * width + core) * rows + row_in
    chosen = (wanted == natural_row(lax.broadcasted_iota(I32, (heads * slot, size), 1), odd)) & (row_in < rows)
    picked = dot(jnp.where(chosen, 1.0, 0.0).astype(BF16), rounded, ((1,), (0,)))
    _, row_in = slot_of(lax.broadcasted_iota(I32, (heads * slot, 1), 0), slot)
    picked = jnp.where(row_in == rows, ratio_high, jnp.where(row_in == rows + 1, ratio - ratio_high, picked))
    tile = [picked[:, t * LANES : (t + 1) * LANES] for t in range(9)]
    low = low_lanes(heads * slot)
    order = [tile[0], tile[1], tile[3], tile[4], tile[7], tile[8], jnp.where(low, tile[2], tile[6]), tile[5]]
    for b in range(heads):
        pay[b] = jnp.concatenate([part[b * slot : (b + 1) * slot] for part in order], axis=0).astype(BF16)
    for i, k in enumerate(FAR + NEAR):
        cut = layers[i].shape[0]
        outs[i][0:cut] = layers[i][...]
        outs[i][cut:] = pay[chip ^ k]


def unpack(width, heads, rows, slot, tokens, *refs):
    pieces = refs[:heads]
    fw_ref, layer_hbm, new_hbm, momentum_hbm, buf, layer_ref, new_ref, momentum_ref, sems = refs[heads:]
    chip, _ = chip_core(width)
    matrix = fw_ref.shape[1] // 3
    for i, k in enumerate(OUT_ORDER):
        buf[chip ^ k] = pieces[i][...]
    mid = tokens // 2
    cut = 2 * tokens + mid
    low = low_lanes(mid)
    low_r = low_lanes(slot)

    def write(lane, block):
        moment = block[0:rows]
        factor = block[rows : rows + 1] + block[rows + 1 : rows + 2]
        momentum_ref[:, lane : lane + LANES] = moment
        new_ref[:, lane : lane + LANES] = (fw_ref[:, lane : lane + LANES] - moment) * factor

    moments = [buf[head, cut:].astype(F32) for head in range(heads)]
    for head in range(heads):
        whole, half = tiles_of(head)
        for m in range(3):
            for t in range(2):
                write(m * matrix + whole + t * LANES, moments[head][(2 * m + t) * slot : (2 * m + t + 1) * slot])
    for head in range(0, heads, 2):
        _, half = tiles_of(head)
        even = moments[head][6 * slot : 7 * slot]
        odd = moments[head + 1][6 * slot : 7 * slot]
        write(half, jnp.where(low_r, even, turned(odd)))
        write(2 * matrix + half, jnp.where(low_r, turned(even), odd))
        even = moments[head][7 * slot :]
        odd = moments[head + 1][7 * slot :]
        write(matrix + half, jnp.where(low_r, even, turned(odd)))
    writes = copy_all([(new_ref, new_hbm), (momentum_ref, momentum_hbm)], sems)
    for head in range(heads):
        whole, half = tiles_of(head)
        layer_ref[:, whole : whole + LANES] = buf[head, 0:tokens]
        layer_ref[:, whole + LANES : whole + 2 * LANES] = buf[head, tokens : 2 * tokens]
    for head in range(0, heads, 2):
        _, half = tiles_of(head)
        even = buf[head, 2 * tokens : cut].astype(F32)
        odd = buf[head + 1, 2 * tokens : cut].astype(F32)
        layer_ref[0:mid, half : half + LANES] = jnp.where(low, turned(even), odd).astype(BF16)
        layer_ref[mid:, half : half + LANES] = jnp.where(low, even, turned(odd)).astype(BF16)
    for copy in writes + copy_all([(layer_ref, layer_hbm)], sems.at[pl.ds(2, 1)]):
        copy.wait()


def shards(queries, key_vectors, value_vectors, step_sizes, fast_weights, fast_gain, window_gain):
    tokens = queries.shape[0]
    heads = step_sizes.shape[1]
    few = heads // 2
    head_width = queries.shape[1] // heads
    scale = 1.0 / math.sqrt(head_width)
    count = lax.axis_size("seq")
    width = count // heads
    rows = fast_weights.shape[0]
    slot = -(-(rows + 3) // 8) * 8
    span = WINDOW // tokens
    wide = 3 * LANES
    slab = few * head_width
    sem = pltpu.SemaphoreType.DMA
    key_rows = 5 * tokens + 4 * slot
    query_rows = 2 * tokens + tokens // 2
    out_rows = query_rows + 8 * slot

    def across(value, step):
        return lax.ppermute(value, "seq", [(i, i ^ step) for i in range(count)])

    def exchange(pieces, steps):
        return [across(piece, k * width) if k else piece for piece, k in zip(pieces, steps)]

    def packed(size, many):
        return [jax.ShapeDtypeStruct((size, LANES), BF16)] * many

    def cost(micros):
        return pl.CostEstimate(flops=micros * 500_000_000, transcendentals=0, bytes_accessed=micros * 2_000_000)

    def call(body, name, micros, *operands, grant=VMEM_LIMIT, **kwargs):
        params = pltpu.CompilerParams(vmem_limit_bytes=grant)
        return pl.pallas_call(
            body, compiler_params=params, cost_estimate=cost(micros), name=name, **kwargs
        )(*operands)

    step_rows = step_sizes.T

    def keys_for(steps):
        return call(
            functools.partial(pack_keys, width, heads, rows, slot, steps),
            "pack_keys",
            2,
            key_vectors,
            value_vectors,
            step_rows,
            fast_weights,
            grant=FULL_VMEM if steps == FAR else VMEM_LIMIT,
            out_shape=packed(key_rows, few),
            in_specs=[HBM] * 4,
            out_specs=[VMEM] * few,
            scratch_shapes=[
                pltpu.VMEM((tokens, slab), BF16),
                pltpu.VMEM((tokens, slab), BF16),
                pltpu.VMEM((heads, tokens), F32),
                pltpu.VMEM((3, rows, slab), F32),
                pltpu.VMEM((few, key_rows, LANES), BF16),
                pltpu.VMEM((few, 8 * slot, LANES), F32),
                sem((6,)),
            ],
        )

    key_pieces = dict(zip(BOTH, keys_for(FAR) + keys_for(NEAR)))
    key_blocks = exchange([key_pieces[k] for k in KEY_ORDER], KEY_ORDER)
    for other in range(1, width):
        key_blocks = key_blocks + [across(block, other) for block in key_blocks[:heads]]
    shared = call(
        functools.partial(pack_weights, heads, tokens),
        "pack_weights",
        0,
        *key_blocks[:heads],
        out_shape=jax.ShapeDtypeStruct((heads * 4 * slot, LANES), BF16),
        in_specs=[VMEM] * heads,
        out_specs=VMEM,
    )
    shared = lax.ppermute(shared, "groups", [(i, i ^ 1) for i in range(lax.axis_size("groups"))])
    shared = [shared] + [across(shared, other) for other in range(1, width)]
    query_pieces = call(
        functools.partial(pack_queries, width, heads),
        "pack_queries",
        1,
        queries,
        out_shape=packed(query_rows, heads),
        in_specs=[VMEM],
        out_specs=[VMEM] * heads,
        scratch_shapes=[pltpu.VMEM((heads, query_rows, LANES), BF16)],
    )
    query_blocks = exchange(query_pieces, FAR + NEAR)

    gradient, copies, key_values = call(
        functools.partial(key_side, width, heads, rows, slot, tokens, scale),
        "key_side",
        0,
        *key_blocks,
        *shared,
        out_shape=[
            jax.ShapeDtypeStruct((head_width, 3 * wide), F32),
            jax.ShapeDtypeStruct((wide, 3 * wide), BF16),
            jax.ShapeDtypeStruct((count, 5 * tokens, LANES), BF16),
        ],
        in_specs=[VMEM] * (count + width),
        out_specs=[VMEM] * 3,
        scratch_shapes=[
            pltpu.VMEM((heads * tokens, 2 * wide), BF16),
            pltpu.VMEM((heads * tokens, wide), BF16),
            pltpu.VMEM((heads * tokens, wide), BF16),
        ],
    )
    gradients = [across(gradient, other) for other in range(1, width)]

    head = lax.axis_index("seq") // width
    odd = head % 2

    def gain_row(gain):
        row = lax.dynamic_slice_in_dim(gain.reshape(heads, head_width), head, 1, 0)
        gap = jnp.zeros((1, HALF), F32)
        even_row = jnp.concatenate([gap, row[:, 2 * LANES :], row[:, : 2 * LANES]], axis=1)
        odd_row = jnp.concatenate([gap, row], axis=1)
        return jnp.where(odd == 1, odd_row, even_row)

    gains = (gain_row(fast_gain), gain_row(window_gain))

    def layers_of(steps, blocks, micros):
        return call(
            functools.partial(query_side, width, heads, tokens, scale, span, steps),
            "query_side",
            micros,
            key_values,
            copies,
            *gains,
            *blocks,
            out_shape=packed(query_rows, few),
            in_specs=[VMEM] * (4 + few),
            out_specs=[VMEM] * few,
            scratch_shapes=[
                pltpu.VMEM((few, query_rows, LANES), BF16),
                pltpu.VMEM((few, query_rows, LANES), BF16),
            ],
        )

    near_layers = layers_of(NEAR, query_blocks[few:], 0)
    far_layers = layers_of(FAR, query_blocks[:few], 40)
    pieces = call(
        functools.partial(pack_momentum, width, heads, rows, slot),
        "pack_momentum",
        2,
        gradient,
        *gradients,
        copies,
        *far_layers,
        *near_layers,
        out_shape=packed(out_rows, heads),
        in_specs=[VMEM] * (width + 1 + heads),
        out_specs=[VMEM] * heads,
        scratch_shapes=[pltpu.VMEM((heads, 8 * slot, LANES), BF16)],
    )
    pieces = dict(zip(BOTH, pieces))
    pieces = exchange([pieces[k] for k in OUT_ORDER], OUT_ORDER)

    return tuple(
        call(
            functools.partial(unpack, width, heads, rows, slot, tokens),
            "unpack",
            2,
            *pieces,
            fast_weights,
            out_shape=[
                jax.ShapeDtypeStruct(queries.shape, BF16),
                jax.ShapeDtypeStruct(fast_weights.shape, F32),
                jax.ShapeDtypeStruct(fast_weights.shape, F32),
            ],
            in_specs=[VMEM] * (heads + 1),
            out_specs=[HBM] * 3,
            scratch_shapes=[
                pltpu.VMEM((heads, out_rows, LANES), BF16),
                pltpu.VMEM(queries.shape, BF16),
                pltpu.VMEM(fast_weights.shape, F32),
                pltpu.VMEM(fast_weights.shape, F32),
                sem((3,)),
            ],
        )
    )


def solution(mesh):
    in_specs = (
        P(("groups", "seq"), None),
        P(("groups", "seq"), None),
        P(("groups", "seq"), None),
        P(("groups", "seq"), None),
        P("seq", None),
        P(),
        P(),
    )
    out_specs = (P(("groups", "seq"), None), P(("groups", "seq"), None), P(("groups", "seq"), None))
    return jax.shard_map(shards, mesh=mesh, in_specs=in_specs, out_specs=out_specs, check_vma=False)
```

```python
import functools
import math

import jax
import jax.numpy as jnp
from jax import lax
from jax.experimental import pallas as pl
from jax.experimental.pallas import tpu as pltpu
from jax.sharding import PartitionSpec as P

WINDOW = 1024
LANES = 128
HALF = 64
VMEM_LIMIT = 24 * 1024 * 1024
FULL_VMEM = 58 * 1024 * 1024
BF16 = jnp.bfloat16
F32 = jnp.float32
I32 = jnp.int32
FAR = (4, 5, 6, 7)
NEAR = (2, 3, 1, 0)
BOTH = FAR + NEAR
KEY_ORDER = (7, 5, 2, 3, 1, 4, 6, 0)
OUT_ORDER = (4, 5, 2, 3, 1, 6, 7, 0)
HBM = pl.BlockSpec(memory_space=pltpu.HBM)
ANY = pl.BlockSpec(memory_space=pl.ANY)
VMEM = pl.BlockSpec(memory_space=pltpu.VMEM)


def tiles_of(head):
    first = (5 * head) // 2
    odd = head % 2
    return (first + odd) * LANES, (first if odd else first + 2) * LANES


def turned(tile):
    return pltpu.roll(tile, HALF, axis=1)


def low_lanes(rows):
    return lax.broadcasted_iota(I32, (rows, LANES), 1) < HALF


def dot(left, right, contract):
    return lax.dot_general(left, right, (contract, ((), ())), preferred_element_type=F32)


def chip_core(width):
    place = lax.axis_index("seq")
    return place // width, lax.rem(place, width)


def slot_of(index, slot):
    part = (index * (65536 // slot + (65536 % slot > 0))) >> 16
    return part, index - part * slot


def natural_row(row, odd):
    return jnp.where(odd == 1, jnp.where(row < 2 * LANES, row + HALF, row - 2 * LANES), row)


def copy_all(pairs, sems):
    copies = [pltpu.make_async_copy(src, dst, sems.at[i]) for i, (src, dst) in enumerate(pairs)]
    for copy in copies:
        copy.start()
    return copies


def pack_keys(width, heads, rows, slot, steps, k_hbm, v_hbm, step_hbm, fw_hbm, *rest):
    few = heads // 2
    outs, (k_ref, v_ref, step_ref, fw_ref, pay, wbuf, sems) = rest[:few], rest[few:]
    chip, _ = chip_core(width)
    side = (chip ^ steps[0]) // few
    slab = k_ref.shape[1]
    matrix = fw_hbm.shape[1] // 3
    at = pl.multiple_of(side * slab, LANES)
    pairs = [(k_hbm.at[:, pl.ds(at, slab)], k_ref), (v_hbm.at[:, pl.ds(at, slab)], v_ref), (step_hbm, step_ref)]
    for m in range(3):
        lane = pl.multiple_of(side * slab + m * matrix, LANES)
        pairs.append((fw_hbm.at[:, pl.ds(lane, slab)], fw_ref.at[m]))
    copies = copy_all(pairs, sems)
    tokens = k_ref.shape[0]
    low = low_lanes(tokens)
    low_r = low_lanes(rows)
    share = pl.multiple_of(lax.rem(lax.axis_index("groups"), 2) * (4 * slot), 8)
    for copy in copies:
        copy.wait()
    wbuf[...] = jnp.zeros_like(wbuf)
    for head in range(few):
        whole, half = tiles_of(head)
        odd = head % 2
        pay[head, 0:tokens] = k_ref[:, whole : whole + LANES]
        pay[head, tokens : 2 * tokens] = k_ref[:, whole + LANES : whole + 2 * LANES]
        pay[head, 3 * tokens : 4 * tokens] = v_ref[:, whole : whole + LANES]
        pay[head, 4 * tokens : 5 * tokens] = v_ref[:, whole + LANES : whole + 2 * LANES]
        k_half = k_ref[:, half : half + LANES].astype(F32)
        v_half = v_ref[:, half : half + LANES].astype(F32)
        mixed = jnp.where(low, turned(k_half) if odd else k_half, v_half if odd else turned(v_half))
        pay[head, 2 * tokens : 3 * tokens] = mixed.astype(BF16)
        halves = []
        for m in range(3):
            for t in range(2):
                spot = (2 * m + t) * slot
                wbuf[head, spot : spot + rows] = fw_ref[m, :, whole + t * LANES : whole + (t + 1) * LANES]
            halves.append(fw_ref[m, :, half : half + LANES])
        first, third, second = halves
        if odd:
            first, third = turned(first), turned(third)
        else:
            second = turned(second)
        wbuf[head, 6 * slot : 6 * slot + rows] = jnp.where(low_r, first, second)
        wbuf[head, 7 * slot : 7 * slot + rows] = jnp.where(low_r, third, 0.0)
        step = step_ref[pl.ds(side * few + head, 1)]
        high = step.astype(BF16).astype(F32)
        middle = (step - high).astype(BF16).astype(F32)
        wbuf[head, pl.ds(share + rows, 1)] = high
        wbuf[head, pl.ds(share + rows + 1, 1)] = middle
        wbuf[head, pl.ds(share + rows + 2, 1)] = step - high - middle
        pay[head, 5 * tokens :] = wbuf[head, pl.ds(share, 4 * slot)].astype(BF16)
    for i, k in enumerate(steps):
        outs[i][...] = pay[lax.rem(chip ^ k, few)]


def pack_queries(width, heads, q_ref, *rest):
    outs, (pay,) = rest[:heads], rest[heads:]
    chip, _ = chip_core(width)
    tokens = q_ref.shape[0]
    mid = tokens // 2
    low = low_lanes(mid)
    for head in range(heads):
        whole, half = tiles_of(head)
        pay[head, 0:tokens] = q_ref[:, whole : whole + LANES]
        pay[head, tokens : 2 * tokens] = q_ref[:, whole + LANES : whole + 2 * LANES]
        top = q_ref[0:mid, half : half + LANES].astype(F32)
        bottom = q_ref[mid:, half : half + LANES].astype(F32)
        if head % 2:
            top = turned(top)
        else:
            bottom = turned(bottom)
        pay[head, 2 * tokens :] = jnp.where(low, top, bottom).astype(BF16)
    for i, k in enumerate(FAR + NEAR):
        outs[i][...] = pay[chip ^ k]


def pack_weights(heads, tokens, *refs):
    ins, out_ref = refs[:heads], refs[heads]
    size = ins[0].shape[0] - 5 * tokens
    for i, k in enumerate(KEY_ORDER):
        out_ref[k * size : (k + 1) * size] = ins[i][5 * tokens :]


def key_side(width, heads, rows, slot, tokens, scale, *refs):
    count = heads * width
    ins = refs[:count]
    shared = refs[count : count + width]
    grad_ref, copy_ref, kv_ref = refs[count + width : count + width + 3]
    gates, hidden, target = refs[count + width + 3 :]
    chip, core = chip_core(width)
    odd = lax.rem(chip, 2)
    wide = 3 * LANES
    size = rows * count
    place = {k: i for i, k in enumerate(KEY_ORDER)}
    blocks = [ins[other * heads + place[k]] for other in range(width) for k in range(heads)]
    for index, block in enumerate(blocks):
        other, k = divmod(index, heads)
        kv_ref[(chip ^ k) * width + (core ^ other)] = block[0 : 5 * tokens]
    parts = [block[5 * tokens :].astype(F32) for block in blocks]
    column, row_in = slot_of(lax.broadcasted_iota(I32, (wide, count * slot), 1), slot)
    source = ((column & (heads - 1)) ^ chip) * width + (core ^ (column >> (heads.bit_length() - 1)))
    wanted = lax.broadcasted_iota(I32, (wide, count * slot), 0)
    chosen = (source * rows + row_in == natural_row(wanted, odd)) & (row_in < rows) & (wanted < size)
    chosen = jnp.where(chosen, 1.0, 0.0).astype(BF16)
    size_4 = 4 * slot
    others = [shared[i // heads][(i % heads) * size_4 : (i % heads + 1) * size_4].astype(F32) for i in range(count)]
    gathered = [
        jnp.concatenate([part[t * slot : (t + 1) * slot] for part in source], axis=0).astype(BF16)
        for source in (parts, others)
        for t in range(4)
    ]
    placed = dot(chosen, jnp.concatenate(gathered, axis=1), ((1,), (0,)))
    mine, theirs = placed[:, : 4 * LANES], placed[:, 4 * LANES :]
    first_share = lax.rem(lax.axis_index("groups"), 2) == 0
    tile = [jnp.where(first_share, mine, theirs), jnp.where(first_share, theirs, mine)]
    tile = [part[:, t * LANES : (t + 1) * LANES] for part in tile for t in range(4)]
    low = low_lanes(wide)
    columns = [tile[0], tile[1], jnp.where(low, tile[6], 0.0), tile[2], tile[3], tile[7]]
    columns += [jnp.where(low, 0.0, tile[6]), tile[4], tile[5]]
    for t, column_tile in enumerate(columns):
        copy_ref[:, t * LANES : (t + 1) * LANES] = column_tile.astype(BF16)

    steps = [jnp.sum(part[rows : rows + 3], axis=0, keepdims=True) for part in parts[:heads]]
    steps = jnp.concatenate(steps, axis=0).T
    w13 = copy_ref[:, 0 : 2 * wide]
    w2 = copy_ref[:, 2 * wide :]
    for j in range(heads):
        block = blocks[j]
        keys = jnp.concatenate([block[t * tokens : (t + 1) * tokens] for t in range(3)], axis=1)
        values = jnp.concatenate([block[t * tokens : (t + 1) * tokens] for t in range(2, 5)], axis=1)
        at = j * tokens
        tgt = (-steps[:, j : j + 1] * values.astype(F32)).astype(BF16)
        both = dot(keys, w13, ((1,), (0,))) * scale
        back = dot(tgt, w2, ((1,), (1,))) * scale
        gate, up = both[:, :wide], both[:, wide:]
        sig = 0.5 + 0.5 * jnp.tanh(0.5 * gate)
        silu = gate * sig
        gates[at : at + tokens, 0:wide] = (back * up * (sig * (1.0 + gate * (1.0 - sig)))).astype(BF16)
        gates[at : at + tokens, wide:] = (back * silu).astype(BF16)
        hidden[at : at + tokens] = (silu * up).astype(BF16)
        target[at : at + tokens] = tgt
    all_keys = [
        jnp.concatenate([blocks[j][t * tokens : (t + 1) * tokens] for t in range(3)], axis=1) for j in range(heads)
    ]
    grads13 = dot(jnp.concatenate(all_keys, axis=0), gates[...], ((0,), (0,))) * scale
    grads2 = dot(hidden[...], target[...], ((0,), (0,))) * scale
    grad_ref[:, 0 : 2 * wide] = grads13[0:size]
    grad_ref[:, 2 * wide :] = grads2[0:size]


def query_side(width, heads, tokens, scale, span, steps, *refs):
    few = heads // 2
    kv_ref, copy_ref, fast_gain_ref, window_gain_ref = refs[:4]
    qs = refs[4 : 4 + few]
    outs, (qbuf, pay) = refs[-(few + 2) : -2], refs[-2:]
    chip, core = chip_core(width)
    for i, k in enumerate(steps):
        qbuf[lax.rem(chip ^ k, few)] = qs[i][...]
    wide = 3 * LANES
    mid = tokens // 2
    low = low_lanes(mid)
    high = jnp.logical_not(low_lanes(2 * tokens))
    size = heads * 40

    def query_block(j):
        tail = qbuf[j, 2 * tokens :].astype(F32)
        half = jnp.concatenate([jnp.where(low, tail, 0.0), jnp.where(low, turned(tail), 0.0)], axis=0)
        return jnp.concatenate([qbuf[j, 0:tokens], qbuf[j, tokens : 2 * tokens], half.astype(BF16)], axis=1)

    def two_blocks(j):
        place = j * width + core
        slot = j % few
        q = jnp.concatenate([query_block(slot), query_block(slot + 1)], axis=0)
        blocks = min(width * (j + 2), span + 1 + width)
        start = 0 if blocks == width * (j + 2) else jnp.maximum(place - span, 0)
        keys_seen = blocks * tokens
        seen = kv_ref[pl.ds(start, blocks)]
        tiles = [seen[:, t * tokens : (t + 1) * tokens].reshape(keys_seen, LANES) for t in range(5)]
        row = lax.broadcasted_iota(I32, (2 * tokens, 1), 0)
        row = jnp.where(row < tokens, row, row + (width - 1) * tokens) + (place - start) * tokens
        score = dot(q, jnp.concatenate(tiles[0:3], axis=1), ((1,), (1,)))

        def masked(first, last):
            distance = row - lax.broadcasted_iota(I32, (2 * tokens, (last - first) * tokens), 1) - first * tokens
            allowed = distance >= 0
            if keys_seen > span * tokens:
                allowed = allowed & (distance < span * tokens)
            return jnp.where(allowed, score[:, first * tokens : last * tokens], -jnp.inf)

        whole = (width + 1, span) if keys_seen > span * tokens else (0, width * j)
        if whole[0] < whole[1]:
            parts = [masked(0, whole[0])] if whole[0] else []
            parts += [score[:, whole[0] * tokens : whole[1] * tokens], masked(whole[1], blocks)]
            score = jnp.concatenate(parts, axis=1)
        else:
            score = masked(0, blocks)
        top = jnp.max(score, axis=1, keepdims=True)
        weight = jnp.exp2((score - top) * (scale * math.log2(math.e)))
        total = jnp.sum(weight, axis=1, keepdims=True)
        attended = dot(weight.astype(BF16), jnp.concatenate(tiles[2:5], axis=1), ((1,), (0,)))
        attended = jnp.concatenate([jnp.where(high, attended[:, 0:LANES], 0.0), attended[:, LANES:]], axis=1)
        share = 1.0 / total
        mean_sq = jnp.sum(attended * attended, axis=1, keepdims=True) * (share * share * (1.0 / size))
        window_part = attended * (share * lax.rsqrt(mean_sq + 1e-05)) * window_gain_ref[...]

        both = dot(q, copy_ref[:, 0 : 2 * wide], ((1,), (0,)))
        gate, up = both[:, :wide], both[:, wide:]
        hid = (gate * up * (0.5 * scale * scale) * (1.0 + jnp.tanh(gate * (0.5 * scale)))).astype(BF16)
        out = dot(hid, copy_ref[:, 2 * wide :], ((1,), (0,)))
        mean_sq = jnp.sum(out * out, axis=1, keepdims=True) * (scale * scale / size)
        layer = out * (scale * lax.rsqrt(mean_sq + 1e-05)) * fast_gain_ref[...] + window_part
        for i in range(2):
            part = layer[i * tokens : (i + 1) * tokens]
            pay[slot + i, 0:tokens] = part[:, LANES : 2 * LANES].astype(BF16)
            pay[slot + i, tokens : 2 * tokens] = part[:, 2 * LANES :].astype(BF16)
            pay[slot + i, 2 * tokens :] = jnp.where(
                low, turned(part[mid:, 0:LANES]), part[0:mid, 0:LANES]
            ).astype(BF16)

    first_half = (chip ^ steps[0]) < few

    @pl.when(first_half)
    def _():
        for j in range(0, few, 2):
            two_blocks(j)

    @pl.when(jnp.logical_not(first_half))
    def _():
        for j in range(few, heads, 2):
            two_blocks(j)

    for i, k in enumerate(steps):
        outs[i][...] = pay[lax.rem(chip ^ k, few)]


def pack_momentum(width, heads, rows, slot, *refs):
    grads = refs[:width]
    copy_ref = refs[width]
    layers = refs[width + 1 : width + 1 + heads]
    outs = refs[width + 1 + heads : width + 1 + 2 * heads]
    pay, wbuf = refs[width + 1 + 2 * heads :]
    chip, core = chip_core(width)
    odd = lax.rem(chip, 2)
    size = rows * heads * width
    wide = 3 * LANES
    summed = grads[0][...]
    for other in grads[1:]:
        summed = summed + other[...]
    rounded = summed.astype(BF16)
    old = copy_ref[0:size].astype(F32)
    moved = old - rounded.astype(F32)
    ratio = (jnp.sum(old * old, axis=0, keepdims=True) + 1e-06) / (jnp.sum(moved * moved, axis=0, keepdims=True) + 1e-06)
    ratio = jnp.sqrt(ratio)
    ratio_high = ratio.astype(BF16).astype(F32)
    head, row_in = slot_of(lax.broadcasted_iota(I32, (heads * slot, size), 0), slot)
    wanted = (head * width + core) * rows + row_in
    chosen = (wanted == natural_row(lax.broadcasted_iota(I32, (heads * slot, size), 1), odd)) & (row_in < rows)
    picked = dot(jnp.where(chosen, 1.0, 0.0).astype(BF16), rounded, ((1,), (0,)))
    _, row_in = slot_of(lax.broadcasted_iota(I32, (heads * slot, 1), 0), slot)
    picked = jnp.where(row_in == rows, ratio_high, jnp.where(row_in == rows + 1, ratio - ratio_high, picked))
    tile = [picked[:, t * LANES : (t + 1) * LANES] for t in range(9)]
    low = low_lanes(heads * slot)
    order = [tile[0], tile[1], tile[3], tile[4], tile[7], tile[8], jnp.where(low, tile[2], tile[6]), tile[5]]
    filled = rows + 2
    wbuf[...] = jnp.zeros_like(wbuf)
    for b in range(heads):
        for t, part in enumerate(order):
            wbuf[b, t * filled : (t + 1) * filled] = part[b * slot : b * slot + filled]
        pay[b] = wbuf[b].astype(BF16)
    for i, k in enumerate(FAR + NEAR):
        cut = layers[i].shape[0]
        outs[i][0:cut] = layers[i][...]
        outs[i][cut:] = pay[chip ^ k]


def unpack(width, heads, rows, tokens, *refs):
    pieces = refs[:heads]
    fw_ref, layer_hbm, new_hbm, momentum_hbm, buf, wbuf, layer_ref, new_ref, momentum_ref, sems = refs[heads:]
    chip, _ = chip_core(width)
    matrix = fw_ref.shape[1] // 3
    for i, k in enumerate(OUT_ORDER):
        buf[chip ^ k] = pieces[i][...]
    mid = tokens // 2
    cut = 2 * tokens + mid
    low = low_lanes(mid)
    slot = rows + 2
    low_r = low_lanes(slot)

    def write(lane, block):
        moment = block[0:rows]
        factor = block[rows : rows + 1] + block[rows + 1 : rows + 2]
        momentum_ref[:, lane : lane + LANES] = moment
        new_ref[:, lane : lane + LANES] = (fw_ref[:, lane : lane + LANES] - moment) * factor

    wbuf[...] = buf[:, cut:].astype(F32)
    for head in range(heads):
        whole, half = tiles_of(head)
        for m in range(3):
            for t in range(2):
                write(m * matrix + whole + t * LANES, wbuf[head, (2 * m + t) * slot : (2 * m + t + 1) * slot])
    for head in range(0, heads, 2):
        _, half = tiles_of(head)
        even = wbuf[head, 6 * slot : 7 * slot]
        odd = wbuf[head + 1, 6 * slot : 7 * slot]
        write(half, jnp.where(low_r, even, turned(odd)))
        write(2 * matrix + half, jnp.where(low_r, turned(even), odd))
        even = wbuf[head, 7 * slot : 8 * slot]
        odd = wbuf[head + 1, 7 * slot : 8 * slot]
        write(matrix + half, jnp.where(low_r, even, turned(odd)))
    writes = copy_all([(new_ref, new_hbm), (momentum_ref, momentum_hbm)], sems)
    for head in range(heads):
        whole, half = tiles_of(head)
        layer_ref[:, whole : whole + LANES] = buf[head, 0:tokens]
        layer_ref[:, whole + LANES : whole + 2 * LANES] = buf[head, tokens : 2 * tokens]
    for head in range(0, heads, 2):
        _, half = tiles_of(head)
        even = buf[head, 2 * tokens : cut].astype(F32)
        odd = buf[head + 1, 2 * tokens : cut].astype(F32)
        layer_ref[0:mid, half : half + LANES] = jnp.where(low, turned(even), odd).astype(BF16)
        layer_ref[mid:, half : half + LANES] = jnp.where(low, even, turned(odd)).astype(BF16)
    for copy in writes + copy_all([(layer_ref, layer_hbm)], sems.at[pl.ds(2, 1)]):
        copy.wait()


def shards(queries, key_vectors, value_vectors, step_sizes, fast_weights, fast_gain, window_gain):
    tokens = queries.shape[0]
    heads = step_sizes.shape[1]
    few = heads // 2
    head_width = queries.shape[1] // heads
    scale = 1.0 / math.sqrt(head_width)
    count = lax.axis_size("seq")
    width = count // heads
    rows = fast_weights.shape[0]
    slot = -(-(rows + 3) // 8) * 8
    span = WINDOW // tokens
    wide = 3 * LANES
    slab = few * head_width
    sem = pltpu.SemaphoreType.DMA
    key_rows = 5 * tokens + 4 * slot
    query_rows = 2 * tokens + tokens // 2
    moment_rows = -(-8 * (rows + 2) // 16) * 16
    out_rows = query_rows + moment_rows

    def across(value, step):
        return lax.ppermute(value, "seq", [(i, i ^ step) for i in range(count)])

    def exchange(pieces, steps):
        return [across(piece, k * width) if k else piece for piece, k in zip(pieces, steps)]

    def packed(size, many):
        return [jax.ShapeDtypeStruct((size, LANES), BF16)] * many

    def cost(micros):
        return pl.CostEstimate(flops=micros * 500_000_000, transcendentals=0, bytes_accessed=micros * 2_000_000)

    def call(body, name, micros, *operands, grant=VMEM_LIMIT, **kwargs):
        params = pltpu.CompilerParams(vmem_limit_bytes=grant)
        return pl.pallas_call(
            body, compiler_params=params, cost_estimate=cost(micros), name=name, **kwargs
        )(*operands)

    step_rows = step_sizes.T

    def keys_for(steps):
        return call(
            functools.partial(pack_keys, width, heads, rows, slot, steps),
            "pack_keys",
            2,
            key_vectors,
            value_vectors,
            step_rows,
            fast_weights,
            grant=FULL_VMEM if steps == FAR else VMEM_LIMIT,
            out_shape=packed(key_rows, few),
            in_specs=[HBM] * 4,
            out_specs=[VMEM] * few,
            scratch_shapes=[
                pltpu.VMEM((tokens, slab), BF16),
                pltpu.VMEM((tokens, slab), BF16),
                pltpu.VMEM((heads, tokens), F32),
                pltpu.VMEM((3, rows, slab), F32),
                pltpu.VMEM((few, key_rows, LANES), BF16),
                pltpu.VMEM((few, 8 * slot, LANES), F32),
                sem((6,)),
            ],
        )

    key_pieces = dict(zip(BOTH, keys_for(FAR) + keys_for(NEAR)))
    key_blocks = exchange([key_pieces[k] for k in KEY_ORDER], KEY_ORDER)
    for other in range(1, width):
        key_blocks = key_blocks + [across(block, other) for block in key_blocks[:heads]]
    shared = call(
        functools.partial(pack_weights, heads, tokens),
        "pack_weights",
        0,
        *key_blocks[:heads],
        out_shape=jax.ShapeDtypeStruct((heads * 4 * slot, LANES), BF16),
        in_specs=[VMEM] * heads,
        out_specs=VMEM,
    )
    shared = lax.ppermute(shared, "groups", [(i, i ^ 1) for i in range(lax.axis_size("groups"))])
    shared = [shared] + [across(shared, other) for other in range(1, width)]
    query_pieces = call(
        functools.partial(pack_queries, width, heads),
        "pack_queries",
        1,
        queries,
        out_shape=packed(query_rows, heads),
        in_specs=[VMEM],
        out_specs=[VMEM] * heads,
        scratch_shapes=[pltpu.VMEM((heads, query_rows, LANES), BF16)],
    )
    query_blocks = exchange(query_pieces, FAR + NEAR)

    gradient, copies, key_values = call(
        functools.partial(key_side, width, heads, rows, slot, tokens, scale),
        "key_side",
        0,
        *key_blocks,
        *shared,
        out_shape=[
            jax.ShapeDtypeStruct((head_width, 3 * wide), F32),
            jax.ShapeDtypeStruct((wide, 3 * wide), BF16),
            jax.ShapeDtypeStruct((count, 5 * tokens, LANES), BF16),
        ],
        in_specs=[VMEM] * (count + width),
        out_specs=[VMEM] * 3,
        scratch_shapes=[
            pltpu.VMEM((heads * tokens, 2 * wide), BF16),
            pltpu.VMEM((heads * tokens, wide), BF16),
            pltpu.VMEM((heads * tokens, wide), BF16),
        ],
    )
    gradients = [across(gradient, other) for other in range(1, width)]

    head = lax.axis_index("seq") // width
    odd = head % 2

    def gain_row(gain):
        row = lax.dynamic_slice_in_dim(gain.reshape(heads, head_width), head, 1, 0)
        gap = jnp.zeros((1, HALF), F32)
        even_row = jnp.concatenate([gap, row[:, 2 * LANES :], row[:, : 2 * LANES]], axis=1)
        odd_row = jnp.concatenate([gap, row], axis=1)
        return jnp.where(odd == 1, odd_row, even_row)

    gains = (gain_row(fast_gain), gain_row(window_gain))

    def layers_of(steps, blocks, micros):
        return call(
            functools.partial(query_side, width, heads, tokens, scale, span, steps),
            "query_side",
            micros,
            key_values,
            copies,
            *gains,
            *blocks,
            out_shape=packed(query_rows, few),
            in_specs=[VMEM] * (4 + few),
            out_specs=[VMEM] * few,
            scratch_shapes=[
                pltpu.VMEM((few, query_rows, LANES), BF16),
                pltpu.VMEM((few, query_rows, LANES), BF16),
            ],
        )

    near_layers = layers_of(NEAR, query_blocks[few:], 0)
    far_layers = layers_of(FAR, query_blocks[:few], 40)
    pieces = call(
        functools.partial(pack_momentum, width, heads, rows, slot),
        "pack_momentum",
        2,
        gradient,
        *gradients,
        copies,
        *far_layers,
        *near_layers,
        out_shape=packed(out_rows, heads),
        in_specs=[VMEM] * (width + 1 + heads),
        out_specs=[VMEM] * heads,
        scratch_shapes=[
            pltpu.VMEM((heads, moment_rows, LANES), BF16),
            pltpu.VMEM((heads, moment_rows, LANES), F32),
        ],
    )
    pieces = dict(zip(BOTH, pieces))
    pieces = exchange([pieces[k] for k in OUT_ORDER], OUT_ORDER)

    return tuple(
        call(
            functools.partial(unpack, width, heads, rows, tokens),
            "unpack",
            2,
            *pieces,
            fast_weights,
            out_shape=[
                jax.ShapeDtypeStruct(queries.shape, BF16),
                jax.ShapeDtypeStruct(fast_weights.shape, F32),
                jax.ShapeDtypeStruct(fast_weights.shape, F32),
            ],
            in_specs=[VMEM] * (heads + 1),
            out_specs=[HBM] * 3,
            scratch_shapes=[
                pltpu.VMEM((heads, out_rows, LANES), BF16),
                pltpu.VMEM((heads, moment_rows, LANES), F32),
                pltpu.VMEM(queries.shape, BF16),
                pltpu.VMEM(fast_weights.shape, F32),
                pltpu.VMEM(fast_weights.shape, F32),
                sem((3,)),
            ],
        )
    )


def solution(mesh):
    in_specs = (
        P(("groups", "seq"), None),
        P(("groups", "seq"), None),
        P(("groups", "seq"), None),
        P(("groups", "seq"), None),
        P("seq", None),
        P(),
        P(),
    )
    out_specs = (P(("groups", "seq"), None), P(("groups", "seq"), None), P(("groups", "seq"), None))
    return jax.shard_map(shards, mesh=mesh, in_specs=in_specs, out_specs=out_specs, check_vma=False)
```
